128 devices in a mesh: lon: 16 (over z, x_hi, core), lat: 8 (over y, x_lo).
Axes of the slice: x: 4 (x_hi: 2, x_lo: 2; x = x_hi * 2 + x_lo), y: 4, z: 4, core: 2. Of those that a mesh axis runs over, the one named last changes fastest.
Arguments:
- stream: bfloat16 [192, 144, 4, 512], P('lon', 'lat'), may hold values from -6 to 6
- w_qkv: bfloat16 [2, 512, 1536], replicated, may hold values from -8 to 8
- w_out: bfloat16 [2, 512, 512], replicated, may hold values from -0.25 to 0.25
- w_up: bfloat16 [2, 512, 2048], replicated, may hold values from -0.25 to 0.25
- w_down: bfloat16 [2, 2048, 512], replicated, may hold values from -0.125 to 0.125
- block_gains: float32 [2, 2, 512], replicated, may hold values from 0.1 to 1.9
- merge_gain: float32 [2048], replicated, may hold values from 0.1 to 1.9
- w_merge: bfloat16 [2048, 1024], replicated, may hold values from -0.125 to 0.125
Outputs:
- merged: bfloat16 [96, 72, 4, 1024], P('lon', 'lat')
The draws below stay inside these ranges and needn't reach their ends.
All inputs are finite; a program needn't handle non-finite values.
Results may differ from the reference program's by a relative error of at most 0.022.
Values may be sent and summed in bfloat16 or wider, within the bound.
No kernel may reach another device: no remote copies, remote signals or barrier semaphores. Data moves between devices by JAX's collectives and lax.ppermute only.
A program may use at most 256 MiB of HBM per device.

```python
import jax
import jax.numpy as jnp
from jax import lax

D = 512
FF = 2048
DM = 1024
HEADS = 8
HEAD_DIM = 64
LEV = 4
LAYERS = 2
NLON = 192
NLAT = 144


def draw_w_qkv(key, part):
    key = jax.random.fold_in(key, 7)
    first_key = jax.random.fold_in(key, 0)
    result = jax.random.normal(first_key, (LAYERS, D, 3 * D), jnp.float32) * D ** (-0.5)
    return result.astype(jnp.bfloat16)


def shard_levels(own_key, dims, cuts, smallest, largest):
    gain = 1.0
    for dim, blocks in cuts:
        steps = jax.random.uniform(jax.random.fold_in(jax.random.fold_in(own_key, 6), dim), (blocks,), jnp.float32, smallest / len(cuts), largest / len(cuts))
        gain = gain * jnp.repeat(jnp.exp(steps), dims[dim] // blocks).reshape((-1,) + (1,) * (len(dims) - 1 - dim))
    return gain


def noise(key, shape, width, bound, pieces=(), kind=jnp.bfloat16):
    loudness = shard_levels(key, shape, pieces, -0.22, 0.18) if pieces else 1.0
    values = jax.random.normal(key, shape, jnp.float32) * width * loudness
    return jnp.minimum(jnp.maximum(values, -bound), bound).astype(kind)


def setup_inputs(seed: int = 0) -> dict:
    key_of = jax.random.split(jax.random.key(seed), 9)
    return {
        "stream": noise(key_of[0], (NLON, NLAT, LEV, D), 1.0, 6.0, ((0, 16), (1, 8))),
        "w_qkv": draw_w_qkv(jax.random.fold_in(key_of[8], 71), 0),
        "w_out": noise(key_of[2], (LAYERS, D, D), D ** -0.5, 0.25),
        "w_up": noise(key_of[3], (LAYERS, D, FF), D ** -0.5, 0.25),
        "w_down": noise(key_of[4], (LAYERS, FF, D), FF ** -0.5, 0.125),
        "block_gains": jnp.clip(1.0 + 0.18 * jax.random.normal(key_of[5], (LAYERS, 2, D), jnp.float32), 0.1, 1.9),
        "merge_gain": jnp.clip(1.0 + 0.18 * jax.random.normal(key_of[6], (4 * D,), jnp.float32), 0.1, 1.9),
        "w_merge": noise(key_of[7], (4 * D, DM), (4 * D) ** -0.5, 0.125),
    }


EPSILON = 1e-05

def normalize(values, scale_vec):
    values = values.astype(jnp.float32)
    center = lax.optimization_barrier(jnp.mean(values, axis=-1, keepdims=True))
    spread = lax.optimization_barrier(jnp.mean(jnp.square(values - center), axis=-1, keepdims=True))
    return (values - center) * lax.rsqrt(spread + EPSILON) * scale_vec.astype(jnp.float32)

def to_windows(field):
    columns, lat_rows, levels, features = field.shape
    shaped = field.reshape(columns // 12, 12, lat_rows // 6, 6, levels // 2, 2, features)
    return shaped.transpose(0, 2, 4, 1, 3, 5, 6).reshape(-1, 144, features)

def from_windows(windows, columns, lat_rows, levels):
    features = windows.shape[-1]
    shaped = windows.reshape(columns // 12, lat_rows // 6, levels // 2, 12, 6, 2, features)
    return shaped.transpose(0, 3, 1, 4, 2, 5, 6).reshape(columns, lat_rows, levels, features)

def attend(packed, allowed):
    features = packed.shape[-1] // 3
    win_count = packed.shape[0]
    queries = packed[..., :features].reshape(win_count, 144, HEADS, HEAD_DIM).astype(jnp.float32)
    key_rows = packed[..., features:2 * features].reshape(win_count, 144, HEADS, HEAD_DIM).astype(jnp.float32)
    value_rows = packed[..., 2 * features:].reshape(win_count, 144, HEADS, HEAD_DIM).astype(jnp.float32)
    scores = jnp.einsum('wqhd,wkhd->whqk', queries, key_rows) * HEAD_DIM ** (-0.5)
    scores = jnp.where(allowed[:, None], scores, -1e+30)
    row_peak = lax.optimization_barrier(jnp.max(scores, axis=-1, keepdims=True))
    weights = jnp.exp(scores - row_peak)
    weights = (weights / lax.optimization_barrier(jnp.sum(weights, axis=-1, keepdims=True))).astype(jnp.bfloat16)
    mixed_out = jnp.einsum('whqk,wkhd->wqhd', weights.astype(jnp.float32), value_rows)
    return mixed_out.reshape(win_count, 144, features).astype(jnp.bfloat16)

def finish(stream, attended, w_out, w_up, w_down, gains):
    features = stream.shape[-1]
    flat_in = stream.reshape(-1, features)
    projected = jnp.dot(attended.reshape(-1, features), w_out, preferred_element_type=jnp.float32)
    middle = (flat_in.astype(jnp.float32) + projected).astype(jnp.bfloat16)
    hidden_in = normalize(middle, gains[1]).astype(jnp.bfloat16)
    raised = jnp.dot(hidden_in, w_up, preferred_element_type=jnp.float32)
    active = jax.nn.gelu(raised).astype(jnp.bfloat16)
    lowered = jnp.dot(active, w_down, preferred_element_type=jnp.float32)
    return (middle.astype(jnp.float32) + lowered).astype(jnp.bfloat16).reshape(stream.shape)

def group_block(lon_slab, lat_group, lev_group, w_qkv, w_out, w_up, w_down, gains):
    columns, lat_rows, levels, features = lon_slab.shape
    normed = normalize(lon_slab, gains[0]).astype(jnp.bfloat16)
    packed = jnp.dot(normed.reshape(-1, features), w_qkv, preferred_element_type=jnp.float32)
    packed = packed.astype(jnp.bfloat16).reshape(columns, lat_rows, levels, 3 * features)
    labels = lat_group[None, :, None] * 2 + lev_group[None, None, :]
    labels = jnp.broadcast_to(labels, (columns, lat_rows, levels)).astype(jnp.int32)[..., None]
    label_win = to_windows(labels)[..., 0]
    allowed = label_win[:, :, None] == label_win[:, None, :]
    attended = from_windows(attend(to_windows(packed), allowed), columns, lat_rows, levels)
    return finish(lon_slab, attended, w_out, w_up, w_down, gains)

def whole_block(stream, lat_group, lev_group, w_qkv, w_out, w_up, w_down, gains):
    lon_slabs = stream.reshape(NLON // 12, 12, NLAT, LEV, D)
    result = lax.map(lambda lon_slab: group_block(lon_slab, lat_group, lev_group, w_qkv, w_out, w_up, w_down, gains), lon_slabs)
    return result.reshape(stream.shape)

def merge_patches(stream, merge_gain, w_merge):
    columns, lat_rows, levels, features = stream.shape
    grouped = stream.reshape(columns // 2, 2, lat_rows // 2, 2, levels, features)
    grouped = grouped.transpose(0, 2, 4, 3, 1, 5).reshape(-1, 4 * features)
    normed = normalize(grouped, merge_gain).astype(jnp.bfloat16)
    result = jnp.dot(normed, w_merge, preferred_element_type=jnp.float32).astype(jnp.bfloat16)
    return result.reshape(columns // 2, lat_rows // 2, levels, w_merge.shape[1])

def reference(stream, w_qkv, w_out, w_up, w_down, block_gains, merge_gain, w_merge):
    zero_lat = jnp.zeros((NLAT,), jnp.int32)
    zero_lev = jnp.zeros((LEV,), jnp.int32)
    current = whole_block(stream, zero_lat, zero_lev, w_qkv[0], w_out[0], w_up[0], w_down[0], block_gains[0])
    rolled = jnp.roll(current, (-6, -3, -1), axis=(0, 1, 2))
    lat_group = (jnp.arange(NLAT) >= NLAT - 3).astype(jnp.int32)
    lev_group = (jnp.arange(LEV) == LEV - 1).astype(jnp.int32)
    rolled = whole_block(rolled, lat_group, lev_group, w_qkv[1], w_out[1], w_up[1], w_down[1], block_gains[1])
    current = jnp.roll(rolled, (6, 3, 1), axis=(0, 1, 2))
    return merge_patches(current, merge_gain, w_merge)
```

```python
import functools

import jax
import jax.numpy as jnp
from jax import lax
from jax.experimental import pallas as pl
from jax.experimental.pallas import tpu as pltpu
from jax.sharding import PartitionSpec as P

EPSILON = 1e-05
D = 512
FF = 2048
COLS, ROWS, LEV = 12, 18, 4
HALF = 432
ALL = 864
WIN = 144
F32 = jnp.float32
BF16 = jnp.bfloat16
VMEM_LIMIT = 44 * 1024 * 1024


def norm_rows(values, gain):
    center = jnp.mean(values, axis=-1, keepdims=True)
    off = values - center
    spread = jnp.mean(off * off, axis=-1, keepdims=True)
    return off * lax.rsqrt(spread + EPSILON) * gain


def round_bf16(values):
    return values.astype(BF16).astype(F32)


def mm(a, b):
    return jnp.dot(a, b, preferred_element_type=F32)


def gelu(x):
    inner = 0.7978845608028654 * (x + 0.044715 * (x * x * x))
    return 0.5 * x * (1.0 + jnp.tanh(inner))


def attend_unit(packed_ref, row0, group, mask):
    span = pl.ds(row0, WIN)
    lo = group * 256
    q = packed_ref[span, lo : lo + 256] * jnp.asarray(0.125, BF16)
    k = packed_ref[span, D + lo : D + lo + 256]
    v = packed_ref[span, 2 * D + lo : 2 * D + lo + 256]
    lane = lax.broadcasted_iota(jnp.int32, (WIN, 256), 1) // 64
    zero = jnp.zeros_like(q)
    stacked = jnp.concatenate([jnp.where(lane == h, q, zero) for h in range(4)], axis=0)
    scores = lax.dot_general(k, stacked, (((1,), (1,)), ((), ())), preferred_element_type=F32)
    if mask is not None:
        scores = jnp.where(mask, scores, -1e30)
    peak = jnp.max(scores, axis=0, keepdims=True)
    e = jnp.exp(scores - peak)
    weights = (e * (1.0 / jnp.sum(e, axis=0, keepdims=True))).astype(BF16)
    mixed = lax.dot_general(weights, v, (((0,), (0,)), ((), ())), preferred_element_type=F32)
    out = mixed[0:WIN]
    for h in range(1, 4):
        out = jnp.where(lane == h, mixed[h * WIN : (h + 1) * WIN], out)
    return out


def finish_rows(stream, attended, wo, wu, wd, gain):
    middle = round_bf16(stream + mm(attended, wo[...]))
    hidden_in = norm_rows(middle, gain).astype(BF16)
    total = middle
    for c in range(4):
        raised = mm(hidden_in, wu[:, c * 512 : (c + 1) * 512])
        total = total + mm(gelu(raised).astype(BF16), wd[c * 512 : (c + 1) * 512, :])
    return round_bf16(total)


def put_rows(ref, start, values):
    for j in range(4):
        ref[j, start : start + values.shape[0], :] = values[:, j * 128 : (j + 1) * 128]


def gather_windows(src, dst, levels):
    for w in range(6):
        for j in range(4):
            pieces = [src[j, pl.ds((w % 3) * 288 + level, 72, stride=4), :] for level in levels[w // 3]]
            dst[w * WIN : (w + 1) * WIN, j * 128 : (j + 1) * 128] = jnp.concatenate(pieces, axis=0).astype(BF16)


def windows_attention(packed, att, levels, masks):
    for w in range(6):
        for group in range(2):
            out = attend_unit(packed, w * WIN, group, masks[w])
            for part, level in enumerate(levels[w // 3]):
                for j in range(2):
                    att[group * 2 + j, pl.ds((w % 3) * 288 + level, 72, stride=4), :] = out[
                        part * 72 : (part + 1) * 72, j * 128 : (j + 1) * 128
                    ]


def half_of(ref, which):
    pieces = [ref[j].reshape(ROWS, 48, 128)[:, which * 24 : which * 24 + 24].reshape(HALF, 128) for j in range(4)]
    return jnp.concatenate(pieces, axis=1)


def load(hbm, vmem, sem):
    copy = pltpu.make_async_copy(hbm, vmem, sem)
    copy.start()
    return copy


def first_kernel(x, wqkv_h, wo_h, wu_h, wd_h, gains, first_a, normed_a, x_b, att_b,
                 xs, ns, nw, packed, wqkv, wo, wu, wd, sems):
    copies = [load(h.at[0], v, sems.at[i])
              for i, (h, v) in enumerate(((wqkv_h, wqkv), (wo_h, wo), (wu_h, wu), (wd_h, wd)))]
    for r in range(ROWS):
        for p in range(6):
            pair = jnp.concatenate([x[2 * p, r].astype(F32), x[2 * p + 1, r].astype(F32)], axis=0)
            put_rows(xs, r * 48 + p * 8, pair)
    put_rows(ns, 0, norm_rows(jnp.concatenate([xs[j] for j in range(4)], axis=1), gains[0, 0:1]))
    gather_windows(ns, nw, ((0, 1), (2, 3)))
    copies[0].wait()
    for c in range(3):
        packed[:, c * 512 : (c + 1) * 512] = mm(nw[...], wqkv[:, c * 512 : (c + 1) * 512]).astype(BF16)
    windows_attention(packed, ns, ((0, 1), (2, 3)), [None] * 6)
    x_b[...] = half_of(xs, 1).astype(BF16)
    att_b[...] = half_of(ns, 1).astype(BF16)
    for copy in copies[1:]:
        copy.wait()
    result = finish_rows(half_of(xs, 0), half_of(ns, 0).astype(BF16), wo, wu, wd, gains[0, 1:2])
    first_a[...] = result.astype(BF16)
    normed_a[...] = norm_rows(result, gains[1, 0:1]).astype(BF16)


def second_kernel(x_b, att_b, wo_h, wu_h, wd_h, gains, first_b, normed_b, wo, wu, wd, sems):
    copies = [load(h.at[0], v, sems.at[i]) for i, (h, v) in enumerate(((wo_h, wo), (wu_h, wu), (wd_h, wd)))]
    for copy in copies:
        copy.wait()
    result = finish_rows(x_b[...].astype(F32), att_b[...], wo, wu, wd, gains[0, 1:2])
    first_b[...] = result.astype(BF16)
    normed_b[...] = norm_rows(result, gains[1, 0:1]).astype(BF16)


def third_kernel(bottom, n_b, n_ra, halo, wqkv_h, z_b, z_ra, ns, nw, packed, wqkv, sems):
    copy = load(wqkv_h.at[1], wqkv, sems.at[0])
    for which, ref in enumerate((n_b, n_ra)):
        rows = ref[...].astype(F32).reshape(ROWS, 24, D)
        extra = halo[...].astype(F32)[which * 72 : (which + 1) * 72].reshape(3, 24, D)
        for r in range(ROWS):
            at = r * 48 + which * 24
            put_rows(ns, at, rows[r + 3] if r < 15 else extra[r - 15])
    levels = ((1, 2), (3, 0))
    gather_windows(ns, nw, levels)
    copy.wait()
    for c in range(3):
        packed[:, c * 512 : (c + 1) * 512] = mm(nw[...], wqkv[:, c * 512 : (c + 1) * 512]).astype(BF16)
    key = lax.broadcasted_iota(jnp.int32, (WIN, 4 * WIN), 0)
    query = lax.rem(lax.broadcasted_iota(jnp.int32, (WIN, 4 * WIN), 1), WIN)
    same_level = (key < 72) == (query < 72)
    same_side = ((lax.rem(key, 72) < 36) == (lax.rem(query, 72) < 36)) | (bottom[0] == 0)
    masks = [None, None, same_side, same_level, same_level, same_level & same_side]
    windows_attention(packed, ns, levels, masks)
    z_b[...] = half_of(ns, 0).astype(BF16)
    z_ra[...] = half_of(ns, 1).astype(BF16)


def fourth_kernel(f_a, f_b, att_a, att_b, wo_h, wu_h, wd_h, gains, merge_gain, wm_h, out,
                  wo, wu, wd, wm, sems):
    copies = [load(h, v, sems.at[i]) for i, (h, v) in enumerate(
        ((wo_h.at[1], wo), (wu_h.at[1], wu), (wd_h.at[1], wd), (wm_h, wm)))]
    for copy in copies[:3]:
        copy.wait()
    s_b = finish_rows(f_b[...].astype(F32), att_b[...], wo, wu, wd, gains[1, 1:2]).reshape(9, 2, 3, 8, D)
    s_a = finish_rows(f_a[...].astype(F32), att_a[...], wo, wu, wd, gains[1, 1:2]).reshape(9, 2, 3, 8, D)
    top = lax.broadcasted_iota(jnp.int32, (216, D), 0) % 8 < 4
    parts = []
    for rp in range(2):
        a = s_a[:, rp].reshape(216, D)
        b = s_b[:, rp].reshape(216, D)
        a_turned = pltpu.roll(a.reshape(27, 8, D), 4, 1).reshape(216, D)
        b_turned = pltpu.roll(b.reshape(27, 8, D), 4, 1).reshape(216, D)
        parts.append(jnp.where(top, a, b_turned))
        parts.append(jnp.where(top, a_turned, b))
    center = sum(jnp.sum(p, axis=-1, keepdims=True) for p in parts) * (1.0 / 2048)
    parts = [p - center for p in parts]
    spread = sum(jnp.sum(p * p, axis=-1, keepdims=True) for p in parts) * (1.0 / 2048)
    scale = lax.rsqrt(spread + EPSILON)
    copies[3].wait()
    total = None
    for i, p in enumerate(parts):
        normed = (p * scale * merge_gain[0:1, i * 512 : (i + 1) * 512]).astype(BF16)
        term = mm(normed, wm[i * 512 : (i + 1) * 512, :])
        total = term if total is None else total + term
    out[...] = total.astype(BF16)


ANY = pl.BlockSpec(memory_space=pl.ANY)
VM = pl.BlockSpec(memory_space=pltpu.VMEM)
SM = pl.BlockSpec(memory_space=pltpu.SMEM)
PARAMS = pltpu.CompilerParams(vmem_limit_bytes=VMEM_LIMIT)


def half_shape():
    return jax.ShapeDtypeStruct((HALF, D), BF16)


FINISH_WEIGHTS = [pltpu.VMEM((D, D), BF16), pltpu.VMEM((D, FF), BF16), pltpu.VMEM((FF, D), BF16)]
ATTENTION_SCRATCH = [pltpu.VMEM((4, ALL, 128), F32), pltpu.VMEM((ALL, D), BF16), pltpu.VMEM((ALL, 3 * D), BF16),
                     pltpu.VMEM((D, 3 * D), BF16)]


def call_first(x, w_qkv, w_out, w_up, w_down, gains):
    return pl.pallas_call(
        first_kernel,
        out_shape=[half_shape()] * 4,
        in_specs=[VM, ANY, ANY, ANY, ANY, VM],
        out_specs=[VM] * 4,
        scratch_shapes=[pltpu.VMEM((4, ALL, 128), F32)] + ATTENTION_SCRATCH + FINISH_WEIGHTS
        + [pltpu.SemaphoreType.DMA((4,))],
        compiler_params=PARAMS,
        name="block_one",
    )(x, w_qkv, w_out, w_up, w_down, gains)


def call_second(x_b, att_b, w_out, w_up, w_down, gains):
    return pl.pallas_call(
        second_kernel,
        out_shape=[half_shape()] * 2,
        in_specs=[VM, VM, ANY, ANY, ANY, VM],
        out_specs=[VM] * 2,
        scratch_shapes=FINISH_WEIGHTS + [pltpu.SemaphoreType.DMA((3,))],
        compiler_params=PARAMS,
        cost_estimate=pl.CostEstimate(flops=4_000_000_000, bytes_accessed=6_000_000, transcendentals=900_000),
        name="block_one_rest",
    )(x_b, att_b, w_out, w_up, w_down, gains)


def call_third(bottom, n_b, n_ra, halo, w_qkv):
    return pl.pallas_call(
        third_kernel,
        out_shape=[half_shape()] * 2,
        in_specs=[SM, VM, VM, VM, ANY],
        out_specs=[VM] * 2,
        scratch_shapes=ATTENTION_SCRATCH + [pltpu.SemaphoreType.DMA((1,))],
        compiler_params=PARAMS,
        name="shifted_attention",
    )(bottom, n_b, n_ra, halo, w_qkv)


def call_fourth(f_a, f_b, att_a, att_b, w_out, w_up, w_down, gains, merge_gain, w_merge):
    return pl.pallas_call(
        fourth_kernel,
        out_shape=jax.ShapeDtypeStruct((216, 1024), BF16),
        in_specs=[VM, VM, VM, VM, ANY, ANY, ANY, VM, VM, ANY],
        out_specs=VM,
        scratch_shapes=FINISH_WEIGHTS + [pltpu.VMEM((4 * D, 1024), BF16), pltpu.SemaphoreType.DMA((4,))],
        compiler_params=PARAMS,
        name="block_two_rest",
    )(f_a, f_b, att_a, att_b, w_out, w_up, w_down, gains, merge_gain, w_merge)


def ring(value, axis, by):
    length = lax.axis_size(axis)
    return lax.ppermute(value, axis, [(i, (i + by) % length) for i in range(length)])


def body(stream, w_qkv, w_out, w_up, w_down, block_gains, merge_gain, w_merge):
    bottom = (lax.axis_index("lat") == lax.axis_size("lat") - 1).astype(jnp.int32).reshape(1)
    first_a, normed_a, x_b, att_b = call_first(stream, w_qkv, w_out, w_up, w_down, block_gains)
    normed_ra = ring(normed_a, "lon", -1)
    first_b, normed_b = call_second(x_b, att_b, w_out, w_up, w_down, block_gains)
    halo = ring(jnp.concatenate([normed_b[:72], normed_ra[:72]], axis=0), "lat", -1)
    z_b, z_ra = call_third(bottom, normed_b, normed_ra, halo, w_qkv)
    back = ring(jnp.concatenate([z_b[360:], z_ra[360:]], axis=0), "lat", 1)
    att_b = jnp.concatenate([back[:72], z_b[:360]], axis=0)
    att_a = ring(jnp.concatenate([back[72:], z_ra[:360]], axis=0), "lon", 1)
    out = call_fourth(first_a, first_b, att_a, att_b, w_out, w_up, w_down, block_gains,
                      merge_gain.reshape(1, -1), w_merge)
    out = out.reshape(9, 3, 2, LEV, 1024).transpose(2, 1, 0, 3, 4)
    return out.reshape(6, 9, LEV, 1024)


def solution(mesh):
    return jax.shard_map(
        body,
        mesh=mesh,
        in_specs=(P("lon", "lat", None, None), P(), P(), P(), P(), P(), P(), P()),
        out_specs=P("lon", "lat", None, None),
        check_vma=False,
    )
```

```python
import functools

import jax
import jax.numpy as jnp
from jax import lax
from jax.experimental import pallas as pl
from jax.experimental.pallas import tpu as pltpu
from jax.sharding import PartitionSpec as P

EPSILON = 1e-05
D = 512
FF = 2048
COLS, ROWS, LEV = 12, 18, 4
HALF = 432
ALL = 864
WIN = 144
F32 = jnp.float32
BF16 = jnp.bfloat16
VMEM_LIMIT = 20 * 1024 * 1024


def norm_rows(values, gain):
    center = jnp.mean(values, axis=-1, keepdims=True)
    off = values - center
    spread = jnp.mean(off * off, axis=-1, keepdims=True)
    return off * lax.rsqrt(spread + EPSILON) * gain


def round_bf16(values):
    return values.astype(BF16).astype(F32)


def mm(a, b):
    return jnp.dot(a, b, preferred_element_type=F32)


def gelu(x):
    inner = 0.7978845608028654 * (x + 0.044715 * (x * x * x))
    return 0.5 * x * (1.0 + jnp.tanh(inner))


def attend_unit(packed_ref, row0, count, group, mask):
    span = pl.ds(row0, WIN)
    lo = group * 256
    q = packed_ref[pl.ds(row0, count), lo : lo + 256] * jnp.asarray(0.125, BF16)
    k = packed_ref[span, D + lo : D + lo + 256]
    v = packed_ref[span, 2 * D + lo : 2 * D + lo + 256]
    lane = lax.broadcasted_iota(jnp.int32, (count, 256), 1) // 64
    zero = jnp.zeros_like(q)
    stacked = jnp.concatenate([jnp.where(lane == h, q, zero) for h in range(4)], axis=0)
    scores = lax.dot_general(stacked, k, (((1,), (1,)), ((), ())), preferred_element_type=F32)
    if mask is not None:
        scores = jnp.where(mask, scores, -1e30)
    e = jnp.exp(scores - jnp.max(scores, axis=1, keepdims=True))
    total = jnp.sum(e, axis=1, keepdims=True)
    mixed = mm(e.astype(BF16), v) * (1.0 / total)
    out = mixed[0:count]
    for h in range(1, 4):
        out = jnp.where(lane == h, mixed[h * count : (h + 1) * count], out)
    return out


def finish_rows(stream, attended, wo, wu, wd, gain):
    middle = round_bf16(stream + mm(attended, wo[...]))
    hidden_in = norm_rows(middle, gain).astype(BF16)
    total = middle
    for c in range(4):
        raised = mm(hidden_in, wu[:, c * 512 : (c + 1) * 512])
        total = total + mm(gelu(raised).astype(BF16), wd[c * 512 : (c + 1) * 512, :])
    return round_bf16(total)


def put_rows(ref, start, values):
    for j in range(4):
        ref[j, start : start + values.shape[0], :] = values[:, j * 128 : (j + 1) * 128]


def window_runs(base, levels, first_half):
    if first_half is None:
        return [(base + level, 72) for level in levels]
    return [(base + half * 144 + level, 36) for half in (first_half, 1 - first_half) for level in levels]


def gather_run(src, j, runs):
    return jnp.concatenate([src[j, pl.ds(start, count, stride=4), :] for start, count in runs], axis=0)


def scatter_run(dst, group, runs, out):
    at = 0
    for start, count in runs:
        for j in range(2):
            dst[group * 2 + j, pl.ds(start, count, stride=4), :] = out[at : at + count, j * 128 : (j + 1) * 128]
        at += count


def gather_windows(src, dst, windows):
    for w, runs in enumerate(windows):
        for j in range(4):
            dst[w * WIN : (w + 1) * WIN, j * 128 : (j + 1) * 128] = gather_run(src, j, runs).astype(BF16)


def project(nw, packed, wqkv):
    for c in range(6):
        packed[:, c * 256 : (c + 1) * 256] = mm(nw[...], wqkv[:, c * 256 : (c + 1) * 256]).astype(BF16)


def half_of(ref, which):
    pieces = [ref[j, 0:ALL, :].reshape(ROWS, 48, 128)[:, which * 24 : which * 24 + 24].reshape(HALF, 128) for j in range(4)]
    return jnp.concatenate(pieces, axis=1)


def load(sems, *pairs):
    groups, used = [], 0
    for source, target in pairs:
        rows = target.shape[0]
        parts = 4 if rows >= 512 else 1
        step = rows // parts
        group = []
        for i in range(parts):
            piece = (source.at[pl.ds(i * step, step)], target.at[pl.ds(i * step, step)]) if parts > 1 else (source, target)
            group.append(pltpu.make_async_copy(*piece, sems.at[used]))
            group[-1].start()
            used += 1
        groups.append(group)
    return groups


def wait(*groups):
    for group in groups:
        for copy in group:
            copy.wait()


def lanes(ref):
    return jnp.concatenate([ref[j] for j in range(4)], axis=1)


def take_stream(x, dst, at, rows):
    for r in range(rows):
        for p in range(6):
            pair = jnp.concatenate([x[2 * p, r].astype(F32), x[2 * p + 1, r].astype(F32)], axis=0)
            put_rows(dst, at + r * 48 + p * 8, pair)


PLAIN = [window_runs(i * 288, levels, None) for levels in ((0, 1), (2, 3)) for i in range(3)]


def first_kernel(x_h, wqkv_h, wo_h, wu_h, wd_h, gains_h, first_a, normed_a, x_b, att_b, wo, wu, wd, gains,
                 x, xs, ns, nw, packed, wqkv, sems):
    copies = load(sems, (x_h, x), (gains_h, gains), (wqkv_h.at[0], wqkv), (wo_h.at[0], wo), (wu_h.at[0], wu),
                  (wd_h.at[0], wd))
    wait(*copies[:2])
    take_stream(x, xs, 0, ROWS)
    put_rows(ns, 0, norm_rows(lanes(xs), gains[0, 0:1]))
    gather_windows(ns, nw, PLAIN)
    wait(copies[2])
    project(nw, packed, wqkv)
    for w, runs in enumerate(PLAIN):
        for group in range(2):
            scatter_run(ns, group, runs, attend_unit(packed, w * WIN, WIN, group, None))
    x_b[...] = half_of(xs, 1).astype(BF16)
    att_b[...] = half_of(ns, 1).astype(BF16)
    wait(*copies[3:])
    result = finish_rows(half_of(xs, 0), half_of(ns, 0).astype(BF16), wo, wu, wd, gains[0, 1:2])
    first_a[...] = result.astype(BF16)
    normed_a[...] = norm_rows(result, gains[1, 0:1]).astype(BF16)


BESIDE = [window_runs(side * 288, levels, 1 - side) for levels in ((0, 1), (2, 3)) for side in range(2)]


def halo_kernel(before, after, wqkv_h, wo, wu, wd, gains, halo_a, halo_b, xs, ns, nw, packed, wqkv, sems):
    copies = load(sems, (wqkv_h.at[0], wqkv))
    take_stream(before, xs, 0, 6)
    take_stream(after, xs, 288, 6)
    put_rows(ns, 0, norm_rows(lanes(xs), gains[0, 0:1]))
    gather_windows(ns, nw, BESIDE)
    wait(*copies)
    project(nw, packed, wqkv)
    attended, stream = [], []
    for w, runs in enumerate(BESIDE):
        parts = [attend_unit(packed, w * WIN, 72, group, None) for group in range(2)]
        attended.append(jnp.concatenate(parts, axis=1))
        stream.append(jnp.concatenate([gather_run(xs, j, runs[:2]) for j in range(4)], axis=1))
    result = finish_rows(jnp.concatenate(stream, axis=0), jnp.concatenate(attended, axis=0).astype(BF16),
                         wo, wu, wd, gains[0, 1:2])
    result = norm_rows(result, gains[1, 0:1])
    for w, runs in enumerate(BESIDE):
        for group in range(2):
            scatter_run(ns, group, runs[:2], result[w * 72 : w * 72 + 72, group * 256 : group * 256 + 256])
    near = jnp.concatenate([lanes(ns)[144:288], lanes(ns)[288:432]], axis=0).reshape(6, 48, D)
    halo_a[...] = near[:, 0:24].reshape(144, D).astype(BF16)
    halo_b[...] = near[:, 24:48].reshape(144, D).astype(BF16)


def second_kernel(x_b, att_b, wo, wu, wd, gains, first_b, normed_b):
    result = finish_rows(x_b[...].astype(F32), att_b[...], wo, wu, wd, gains[0, 1:2])
    first_b[...] = result.astype(BF16)
    normed_b[...] = norm_rows(result, gains[1, 0:1]).astype(BF16)


HALVES = (1, None, None, 0)
SHIFTED = [window_runs(i * 288, levels, HALVES[i]) for levels in ((1, 2), (3, 0)) for i in range(4)]


def third_kernel(edge, n_b, n_ra, halo_b, halo_ra, wqkv_h, wo_h, wu_h, wd_h, z_b, z_ra, wo, wu, wd,
                 ns, nw, packed, wqkv, sems):
    copies = load(sems, (wqkv_h.at[1], wqkv), (wo_h.at[1], wo), (wu_h.at[1], wu), (wd_h.at[1], wd))
    for which, (ref, halo) in enumerate(((n_b, halo_b), (n_ra, halo_ra))):
        rows = ref[...].astype(F32).reshape(ROWS, 24, D)
        extra = halo[...].astype(F32).reshape(6, 24, D)
        for r in range(24):
            put_rows(ns, r * 48 + which * 24, rows[r - 3] if 3 <= r < 21 else extra[r if r < 3 else r - 18])
    gather_windows(ns, nw, SHIFTED)
    wait(copies[0])
    project(nw, packed, wqkv)
    for w, runs in enumerate(SHIFTED):
        i, lonely = w % 4, w >= 4
        count = WIN if HALVES[i] is None else 72
        key = lax.broadcasted_iota(jnp.int32, (4 * count, WIN), 1)
        query = lax.rem(lax.broadcasted_iota(jnp.int32, (4 * count, WIN), 0), count)
        mask = None
        if lonely:
            mask = (lax.rem(key, count) < count // 2) == (query < count // 2)
        if count == 72:
            inside = (key < 72) | (edge[i // 3] == 0)
            mask = inside if mask is None else mask & inside
            runs = runs[:2]
        runs = [(start - 144, length) for start, length in runs]
        for group in range(2):
            scatter_run(ns, group, runs, attend_unit(packed, w * WIN, count, group, mask))
    z_b[...] = half_of(ns, 0).astype(BF16)
    z_ra[...] = half_of(ns, 1).astype(BF16)
    wait(*copies[1:])


def fourth_kernel(f_b, att_b, wo, wu, wd, gains, second_b):
    second_b[...] = finish_rows(f_b[...].astype(F32), att_b[...], wo, wu, wd, gains[1, 1:2]).astype(BF16)


def fifth_kernel(f_a, att_a, second_b, wo, wu, wd, gains, mg_h, wm_h, out, merge_gain, wm, sems):
    copies = load(sems, (mg_h, merge_gain), (wm_h, wm))
    s_a = finish_rows(f_a[...].astype(F32), att_a[...], wo, wu, wd, gains[1, 1:2]).reshape(9, 2, 3, 8, D)
    s_b = second_b[...].astype(F32).reshape(9, 2, 3, 8, D)
    top = lax.broadcasted_iota(jnp.int32, (216, D), 0) % 8 < 4
    parts = []
    for rp in range(2):
        a = s_a[:, rp].reshape(216, D)
        b = s_b[:, rp].reshape(216, D)
        a_turned = pltpu.roll(a.reshape(27, 8, D), 4, 1).reshape(216, D)
        b_turned = pltpu.roll(b.reshape(27, 8, D), 4, 1).reshape(216, D)
        parts.append(jnp.where(top, a, b_turned))
        parts.append(jnp.where(top, a_turned, b))
    center = sum(jnp.sum(p, axis=-1, keepdims=True) for p in parts) * (1.0 / 2048)
    parts = [p - center for p in parts]
    spread = sum(jnp.sum(p * p, axis=-1, keepdims=True) for p in parts) * (1.0 / 2048)
    scale = lax.rsqrt(spread + EPSILON)
    wait(copies[0])
    total = None
    for i, p in enumerate(parts):
        copies[1][i].wait()
        normed = (p * scale * merge_gain[0:1, i * 512 : (i + 1) * 512]).astype(BF16)
        term = mm(normed, wm[i * 512 : (i + 1) * 512, :])
        total = term if total is None else total + term
    for j in range(9):
        for i in range(3):
            at = (j * 3 + i) * 8
            out[i, j] = total[at : at + 4].astype(BF16)
            out[3 + i, j] = total[at + 4 : at + 8].astype(BF16)


VM = pl.BlockSpec(memory_space=pltpu.VMEM)


def half(count):
    return [pltpu.VMEM((HALF, D), BF16)] * count


def rows_f32(tokens):
    return pltpu.VMEM((4, tokens, 128), F32)


def attention_scratch(tokens):
    return [rows_f32(tokens), pltpu.VMEM((tokens, D), BF16), pltpu.VMEM((tokens, 3 * D), BF16)]


QKV = [pltpu.VMEM((D, 3 * D), BF16)]
FINISH = [pltpu.VMEM((D, D), BF16), pltpu.VMEM((D, FF), BF16), pltpu.VMEM((FF, D), BF16)]
GAINS = [pltpu.VMEM((2, 2, D), F32)]
MERGE = [pltpu.VMEM((1, 4 * D), F32), pltpu.VMEM((4 * D, 1024), BF16)]


def call(kernel, name, outs, args, scratch, sems, flops):
    values = [pltpu.with_memory_space_constraint(v, pltpu.HBM) if m is pltpu.HBM else v for v, m in args]
    outs = [jax.ShapeDtypeStruct(o.shape, o.dtype) for o in outs]
    return pl.pallas_call(
        kernel,
        out_shape=outs,
        in_specs=[pl.BlockSpec(memory_space=m) for _, m in args],
        out_specs=jax.tree.map(lambda _: VM, outs),
        scratch_shapes=scratch + ([pltpu.SemaphoreType.DMA((4 * sems,))] if sems else []),
        compiler_params=pltpu.CompilerParams(vmem_limit_bytes=VMEM_LIMIT),
        cost_estimate=pl.CostEstimate(flops=flops, bytes_accessed=6_000_000, transcendentals=900_000),
        name=name,
    )(*values)


def hbm(*values):
    return [(v, pltpu.HBM) for v in values]


def vmem(*values):
    return [(v, pltpu.VMEM) for v in values]


def ring(value, axis, by):
    length = lax.axis_size(axis)
    return lax.ppermute(value, axis, [(i, (i + by) % length) for i in range(length)])


def body(stream, w_qkv, w_out, w_up, w_down, gains, merge_gain, w_merge):
    place = lax.axis_index("lat")
    edge = jnp.stack([place == 0, place == lax.axis_size("lat") - 1]).astype(jnp.int32)
    after = ring(stream[:, :6], "lat", -1)
    before = ring(stream[:, 12:], "lat", 1)
    first_a, normed_a, x_b, att_b, wo0, wu0, wd0, gains = call(
        first_kernel, "block_one", half(4) + FINISH + GAINS, hbm(stream, w_qkv, w_out, w_up, w_down, gains),
        [pltpu.VMEM((COLS, ROWS, LEV, D), BF16), rows_f32(ALL)] + attention_scratch(ALL) + QKV, 6, 6_000_000_000)
    normed_ra = ring(normed_a, "lon", -1)
    halo_a, halo_b = call(
        halo_kernel, "block_one_beside", [pltpu.VMEM((144, D), BF16)] * 2,
        vmem(before, after) + hbm(w_qkv) + vmem(wo0, wu0, wd0, gains),
        [rows_f32(576)] + attention_scratch(576) + QKV, 1, 4_000_000_000)
    halo_ra = ring(halo_a, "lon", -1)
    first_b, normed_b = call(
        second_kernel, "block_one_rest", half(2), vmem(x_b, att_b, wo0, wu0, wd0, gains), [], 0, 4_000_000_000)
    z_b, z_ra, wo1, wu1, wd1 = call(
        third_kernel, "shifted_attention", half(2) + FINISH,
        [(edge, pltpu.SMEM)] + vmem(normed_b, normed_ra, halo_b, halo_ra) + hbm(w_qkv, w_out, w_up, w_down),
        attention_scratch(1152) + QKV, 4, 4_000_000_000)
    att_a = ring(z_ra, "lon", 1)
    second_b, = call(
        fourth_kernel, "block_two_rest", half(1), vmem(first_b, z_b, wo1, wu1, wd1, gains), [], 0, 4_000_000_000)
    out, = call(
        fifth_kernel, "merge", [jax.ShapeDtypeStruct((6, 9, LEV, 1024), BF16)],
        vmem(first_a, att_a, second_b, wo1, wu1, wd1, gains) + hbm(merge_gain.reshape(1, -1), w_merge),
        MERGE, 2, 5_000_000_000)
    return out


def solution(mesh):
    return jax.shard_map(
        body,
        mesh=mesh,
        in_specs=(P("lon", "lat", None, None), P(), P(), P(), P(), P(), P(), P()),
        out_specs=P("lon", "lat", None, None),
        check_vma=False,
    )
```

```python
import functools

import jax
import jax.numpy as jnp
from jax import lax
from jax.experimental import pallas as pl
from jax.experimental.pallas import tpu as pltpu
from jax.sharding import PartitionSpec as P

EPSILON = 1e-05
D = 512
FF = 2048
COLS, ROWS, LEV = 12, 18, 4
HALF = 432
ALL = 864
WIN = 144
F32 = jnp.float32
BF16 = jnp.bfloat16
VMEM_LIMIT = 20 * 1024 * 1024


def norm_rows(values, gain):
    center = jnp.mean(values, axis=-1, keepdims=True)
    off = values - center
    spread = jnp.mean(off * off, axis=-1, keepdims=True)
    return off * lax.rsqrt(spread + EPSILON) * gain


def round_bf16(values):
    return values.astype(BF16).astype(F32)


def mm(a, b):
    return jnp.dot(a, b, preferred_element_type=F32)


def gelu(x):
    inner = 0.7978845608028654 * (x + 0.044715 * (x * x * x))
    return 0.5 * x * (1.0 + jnp.tanh(inner))


def attend_unit(packed_ref, row0, count, group, mask):
    span = pl.ds(row0, WIN)
    lo = group * 256
    q = packed_ref[pl.ds(row0, count), lo : lo + 256] * jnp.asarray(0.125, BF16)
    k = packed_ref[span, D + lo : D + lo + 256]
    v = packed_ref[span, 2 * D + lo : 2 * D + lo + 256]
    lane = lax.broadcasted_iota(jnp.int32, (count, 256), 1) // 64
    zero = jnp.zeros_like(q)
    stacked = jnp.concatenate([jnp.where(lane == h, q, zero) for h in range(4)], axis=0)
    scores = lax.dot_general(stacked, k, (((1,), (1,)), ((), ())), preferred_element_type=F32)
    if mask is not None:
        scores = jnp.where(mask, scores, -1e30)
    e = jnp.exp(scores - jnp.max(scores, axis=1, keepdims=True))
    total = jnp.sum(e, axis=1, keepdims=True)
    mixed = mm(e.astype(BF16), v) * (1.0 / total)
    out = mixed[0:count]
    for h in range(1, 4):
        out = jnp.where(lane == h, mixed[h * count : (h + 1) * count], out)
    return out


def finish_rows(stream, attended, wo, wu, wd, gain):
    middle = round_bf16(stream + mm(attended, wo[...]))
    hidden_in = norm_rows(middle, gain).astype(BF16)
    total = middle
    for c in range(4):
        raised = mm(hidden_in, wu[:, c * 512 : (c + 1) * 512])
        total = total + mm(gelu(raised).astype(BF16), wd[c * 512 : (c + 1) * 512, :])
    return round_bf16(total)


def put_rows(ref, start, values):
    for j in range(4):
        ref[j, start : start + values.shape[0], :] = values[:, j * 128 : (j + 1) * 128]


def window_runs(base, levels, first_half):
    if first_half is None:
        return [(base + level, 72) for level in levels]
    return [(base + half * 144 + level, 36) for half in (first_half, 1 - first_half) for level in levels]


def gather_run(src, j, runs):
    return jnp.concatenate([src[j, pl.ds(start, count, stride=4), :] for start, count in runs], axis=0)


def scatter_run(dst, group, runs, out):
    at = 0
    for start, count in runs:
        for j in range(2):
            dst[group * 2 + j, pl.ds(start, count, stride=4), :] = out[at : at + count, j * 128 : (j + 1) * 128]
        at += count


def gather_windows(src, dst, windows):
    for w, runs in enumerate(windows):
        for j in range(4):
            dst[w * WIN : (w + 1) * WIN, j * 128 : (j + 1) * 128] = gather_run(src, j, runs).astype(BF16)


def project(nw, packed, wqkv):
    for c in range(6):
        packed[:, c * 256 : (c + 1) * 256] = mm(nw[...], wqkv[:, c * 256 : (c + 1) * 256]).astype(BF16)


def half_of(ref, which):
    pieces = [ref[j, 0:ALL, :].reshape(ROWS, 48, 128)[:, which * 24 : which * 24 + 24].reshape(HALF, 128) for j in range(4)]
    return jnp.concatenate(pieces, axis=1)


def load(sems, *pairs):
    groups, used = [], 0
    for source, target in pairs:
        rows = target.shape[0]
        parts = 4 if rows >= 512 else 1
        step = rows // parts
        group = []
        for i in range(parts):
            piece = (source.at[pl.ds(i * step, step)], target.at[pl.ds(i * step, step)]) if parts > 1 else (source, target)
            group.append(pltpu.make_async_copy(*piece, sems.at[used]))
            group[-1].start()
            used += 1
        groups.append(group)
    return groups


def wait(*groups):
    for group in groups:
        for copy in group:
            copy.wait()


def lanes(ref):
    return jnp.concatenate([ref[j] for j in range(4)], axis=1)


def take_stream(x, dst, at, rows):
    for r in range(rows):
        for p in range(6):
            pair = jnp.concatenate([x[2 * p, r].astype(F32), x[2 * p + 1, r].astype(F32)], axis=0)
            put_rows(dst, at + r * 48 + p * 8, pair)


PLAIN = [window_runs(i * 288, levels, None) for levels in ((0, 1), (2, 3)) for i in range(3)]


def first_kernel(x_h, wqkv_h, wo_h, wu_h, wd_h, gains_h, first_a, normed_a, x_b, att_b, wqkv, wo, wu, wd, gains,
                 x, xs, ns, nw, packed, sems):
    early = load(sems, (x_h, x), (gains_h, gains), (wqkv_h.at[0], wqkv))
    wait(*early[:2])
    take_stream(x, xs, 0, ROWS)
    put_rows(ns, 0, norm_rows(lanes(xs), gains[0, 0:1]))
    gather_windows(ns, nw, PLAIN)
    wait(early[2])
    copies = load(sems.at[6:], (wo_h.at[0], wo), (wu_h.at[0], wu), (wd_h.at[0], wd))
    project(nw, packed, wqkv)
    for w, runs in enumerate(PLAIN):
        for group in range(2):
            scatter_run(ns, group, runs, attend_unit(packed, w * WIN, WIN, group, None))
    x_b[...] = half_of(xs, 1).astype(BF16)
    att_b[...] = half_of(ns, 1).astype(BF16)
    wait(*copies)
    result = finish_rows(half_of(xs, 0), half_of(ns, 0).astype(BF16), wo, wu, wd, gains[0, 1:2])
    first_a[...] = result.astype(BF16)
    normed_a[...] = norm_rows(result, gains[1, 0:1]).astype(BF16)


BESIDE = [window_runs(side * 288, levels, 1 - side) for levels in ((0, 1), (2, 3)) for side in range(2)]


def halo_kernel(before, after, wqkv, wo, wu, wd, gains, halo_a, halo_b, xs, ns, nw, packed):
    take_stream(before, xs, 0, 6)
    take_stream(after, xs, 288, 6)
    put_rows(ns, 0, norm_rows(lanes(xs), gains[0, 0:1]))
    gather_windows(ns, nw, BESIDE)
    project(nw, packed, wqkv)
    attended, stream = [], []
    for w, runs in enumerate(BESIDE):
        parts = [attend_unit(packed, w * WIN, 72, group, None) for group in range(2)]
        attended.append(jnp.concatenate(parts, axis=1))
        stream.append(jnp.concatenate([gather_run(xs, j, runs[:2]) for j in range(4)], axis=1))
    result = finish_rows(jnp.concatenate(stream, axis=0), jnp.concatenate(attended, axis=0).astype(BF16),
                         wo, wu, wd, gains[0, 1:2])
    result = norm_rows(result, gains[1, 0:1])
    for w, runs in enumerate(BESIDE):
        for group in range(2):
            scatter_run(ns, group, runs[:2], result[w * 72 : w * 72 + 72, group * 256 : group * 256 + 256])
    near = jnp.concatenate([lanes(ns)[144:288], lanes(ns)[288:432]], axis=0).reshape(6, 48, D)
    halo_a[...] = near[:, 0:24].reshape(144, D).astype(BF16)
    halo_b[...] = near[:, 24:48].reshape(144, D).astype(BF16)


def second_kernel(x_b, att_b, wo, wu, wd, gains, first_b, normed_b):
    result = finish_rows(x_b[...].astype(F32), att_b[...], wo, wu, wd, gains[0, 1:2])
    first_b[...] = result.astype(BF16)
    normed_b[...] = norm_rows(result, gains[1, 0:1]).astype(BF16)


HALVES = (1, None, None, 0)
SHIFTED = [window_runs(i * 288, levels, HALVES[i]) for levels in ((1, 2), (3, 0)) for i in range(4)]


def third_kernel(edge, n_b, n_ra, halo_b, halo_ra, wqkv_h, wo_h, wu_h, wd_h, z_b, z_ra, wo, wu, wd,
                 ns, nw, packed, wqkv, sems):
    early = load(sems, (wqkv_h.at[1], wqkv))
    for which, (ref, halo) in enumerate(((n_b, halo_b), (n_ra, halo_ra))):
        rows = ref[...].astype(F32).reshape(ROWS, 24, D)
        extra = halo[...].astype(F32).reshape(6, 24, D)
        for r in range(24):
            put_rows(ns, r * 48 + which * 24, rows[r - 3] if 3 <= r < 21 else extra[r if r < 3 else r - 18])
    copies = load(sems.at[4:], (wo_h.at[1], wo), (wu_h.at[1], wu), (wd_h.at[1], wd))
    gather_windows(ns, nw, SHIFTED)
    wait(*early)
    project(nw, packed, wqkv)
    for w, runs in enumerate(SHIFTED):
        i, lonely = w % 4, w >= 4
        count = WIN if HALVES[i] is None else 72
        key = lax.broadcasted_iota(jnp.int32, (4 * count, WIN), 1)
        query = lax.rem(lax.broadcasted_iota(jnp.int32, (4 * count, WIN), 0), count)
        mask = None
        if lonely:
            mask = (lax.rem(key, count) < count // 2) == (query < count // 2)
        if count == 72:
            inside = (key < 72) | (edge[i // 3] == 0)
            mask = inside if mask is None else mask & inside
            runs = runs[:2]
        runs = [(start - 144, length) for start, length in runs]
        for group in range(2):
            scatter_run(ns, group, runs, attend_unit(packed, w * WIN, count, group, mask))
    z_b[...] = half_of(ns, 0).astype(BF16)
    z_ra[...] = half_of(ns, 1).astype(BF16)
    wait(*copies)


def merge_half(values, gain, wm, landed, out):
    pairs = values[: 8 * 48].reshape(4, 2, 2, 3, 8, D)
    last = values[8 * 48 :].reshape(1, 2, 3, 8, D)
    top = lax.broadcasted_iota(jnp.int32, (120, D), 0) % 8 < 4
    parts = []
    for rp in range(2):
        even = jnp.concatenate([pairs[:, 0, rp], last[:, rp]], axis=0).reshape(15, 8, D)
        odd = jnp.concatenate([pairs[:, 1, rp], last[:, rp]], axis=0).reshape(15, 8, D)
        even_turned = pltpu.roll(even, 4, 1).reshape(120, D)
        odd_turned = pltpu.roll(odd, 4, 1).reshape(120, D)
        parts.append(jnp.where(top, even.reshape(120, D), odd_turned))
        parts.append(jnp.where(top, even_turned, odd.reshape(120, D)))
    center = sum(jnp.sum(p, axis=-1, keepdims=True) for p in parts) * (1.0 / 2048)
    parts = [p - center for p in parts]
    spread = sum(jnp.sum(p * p, axis=-1, keepdims=True) for p in parts) * (1.0 / 2048)
    scale = lax.rsqrt(spread + EPSILON)
    total = None
    for i, p in enumerate(parts):
        normed = (p * scale * gain[0:1, i * 512 : (i + 1) * 512]).astype(BF16)
        landed(i)
        term = mm(normed, wm[i * 512 : (i + 1) * 512, :])
        total = term if total is None else total + term
    for j in range(9):
        for i in range(3):
            at = (j // 2 * 3 + i) * 8 + j % 2 * 4
            out[i, j] = total[at : at + 4].astype(BF16)


def fourth_kernel(f_b, att_b, wo, wu, wd, gains, mg_h, wm_h, out_b, gain, wm, sems):
    copies = load(sems, (mg_h, gain), (wm_h, wm))
    second = finish_rows(f_b[...].astype(F32), att_b[...], wo, wu, wd, gains[1, 1:2])
    wait(copies[0])
    merge_half(second, gain, wm, lambda i: copies[1][i].wait(), out_b)


def fifth_kernel(f_a, att_a, out_b, wo, wu, wd, gains, gain, wm, out):
    second = finish_rows(f_a[...].astype(F32), att_a[...], wo, wu, wd, gains[1, 1:2])
    merge_half(second, gain, wm, lambda i: None, out)
    for i in range(3):
        out[3 + i] = out_b[i]


VM = pl.BlockSpec(memory_space=pltpu.VMEM)


def half(count):
    return [pltpu.VMEM((HALF, D), BF16)] * count


def rows_f32(tokens):
    return pltpu.VMEM((4, tokens, 128), F32)


def attention_scratch(tokens):
    return [rows_f32(tokens), pltpu.VMEM((tokens, D), BF16), pltpu.VMEM((tokens, 3 * D), BF16)]


QKV = [pltpu.VMEM((D, 3 * D), BF16)]
FINISH = [pltpu.VMEM((D, D), BF16), pltpu.VMEM((D, FF), BF16), pltpu.VMEM((FF, D), BF16)]
GAINS = [pltpu.VMEM((2, 2, D), F32)]
MERGE = [pltpu.VMEM((1, 4 * D), F32), pltpu.VMEM((4 * D, 1024), BF16)]


def call(kernel, name, outs, args, scratch, sems, flops):
    values = [pltpu.with_memory_space_constraint(v, pltpu.HBM) if m is pltpu.HBM else v for v, m in args]
    outs = [jax.ShapeDtypeStruct(o.shape, o.dtype) for o in outs]
    return pl.pallas_call(
        kernel,
        out_shape=outs,
        in_specs=[pl.BlockSpec(memory_space=m) for _, m in args],
        out_specs=jax.tree.map(lambda _: VM, outs),
        scratch_shapes=scratch + ([pltpu.SemaphoreType.DMA((4 * sems,))] if sems else []),
        compiler_params=pltpu.CompilerParams(vmem_limit_bytes=VMEM_LIMIT),
        cost_estimate=pl.CostEstimate(flops=flops, bytes_accessed=6_000_000, transcendentals=900_000),
        name=name,
    )(*values)


def hbm(*values):
    return [(v, pltpu.HBM) for v in values]


def vmem(*values):
    return [(v, pltpu.VMEM) for v in values]


def ring(value, axis, by):
    length = lax.axis_size(axis)
    return lax.ppermute(value, axis, [(i, (i + by) % length) for i in range(length)])


def body(stream, w_qkv, w_out, w_up, w_down, gains, merge_gain, w_merge):
    place = lax.axis_index("lat")
    edge = jnp.stack([place == 0, place == lax.axis_size("lat") - 1]).astype(jnp.int32)
    after = ring(stream[:, :6], "lat", -1)
    before = ring(stream[:, 12:], "lat", 1)
    first_a, normed_a, x_b, att_b, wqkv0, wo0, wu0, wd0, gains = call(
        first_kernel, "block_one", half(4) + QKV + FINISH + GAINS, hbm(stream, w_qkv, w_out, w_up, w_down, gains),
        [pltpu.VMEM((COLS, ROWS, LEV, D), BF16), rows_f32(ALL)] + attention_scratch(ALL), 6, 6_000_000_000)
    normed_ra = ring(normed_a, "lon", -1)
    halo_a, halo_b = call(
        halo_kernel, "block_one_beside", [pltpu.VMEM((144, D), BF16)] * 2,
        vmem(before, after, wqkv0, wo0, wu0, wd0, gains), [rows_f32(576)] + attention_scratch(576), 0, 4_000_000_000)
    halo_ra = ring(halo_a, "lon", -1)
    first_b, normed_b = call(
        second_kernel, "block_one_rest", half(2), vmem(x_b, att_b, wo0, wu0, wd0, gains), [], 0, 4_000_000_000)
    z_b, z_ra, wo1, wu1, wd1 = call(
        third_kernel, "shifted_attention", half(2) + FINISH,
        [(edge, pltpu.SMEM)] + vmem(normed_b, normed_ra, halo_b, halo_ra) + hbm(w_qkv, w_out, w_up, w_down),
        attention_scratch(1152) + QKV, 4, 4_000_000_000)
    att_a = ring(z_ra, "lon", 1)
    out_b, mg, wm = call(
        fourth_kernel, "block_two_rest", [jax.ShapeDtypeStruct((3, 9, LEV, 1024), BF16)] + MERGE,
        vmem(first_b, z_b, wo1, wu1, wd1, gains) + hbm(merge_gain.reshape(1, -1), w_merge), [], 2, 5_000_000_000)
    out, = call(
        fifth_kernel, "merge", [jax.ShapeDtypeStruct((6, 9, LEV, 1024), BF16)],
        vmem(first_a, att_a, out_b, wo1, wu1, wd1, gains, mg, wm), [], 0, 5_000_000_000)
    return out


def solution(mesh):
    return jax.shard_map(
        body,
        mesh=mesh,
        in_specs=(P("lon", "lat", None, None), P(), P(), P(), P(), P(), P(), P()),
        out_specs=P("lon", "lat", None, None),
        check_vma=False,
    )
```

```python
import functools

import jax
import jax.numpy as jnp
from jax import lax
from jax.experimental import pallas as pl
from jax.experimental.pallas import tpu as pltpu
from jax.sharding import PartitionSpec as P

EPSILON = 1e-05
D = 512
FF = 2048
COLS, ROWS, LEV = 12, 18, 4
HALF = 432
ALL = 864
WIN = 144
F32 = jnp.float32
BF16 = jnp.bfloat16
VMEM_LIMIT = 20 * 1024 * 1024


def norm_rows(values, gain):
    center = jnp.mean(values, axis=-1, keepdims=True)
    off = values - center
    spread = jnp.mean(off * off, axis=-1, keepdims=True)
    return off * lax.rsqrt(spread + EPSILON) * gain


def round_bf16(values):
    return values.astype(BF16).astype(F32)


def mm(a, b):
    return jnp.dot(a, b, preferred_element_type=F32)


def gelu(x):
    inner = 0.7978845608028654 * (x + 0.044715 * (x * x * x))
    return 0.5 * x * (1.0 + jnp.tanh(inner))


def attend_unit(packed_ref, row0, count, group, mask):
    span = pl.ds(row0, WIN)
    lo = group * 256
    q = packed_ref[pl.ds(row0, count), lo : lo + 256] * jnp.asarray(0.125, BF16)
    k = packed_ref[span, D + lo : D + lo + 256]
    v = packed_ref[span, 2 * D + lo : 2 * D + lo + 256]
    lane = lax.broadcasted_iota(jnp.int32, (count, 256), 1) // 64
    zero = jnp.zeros_like(q)
    stacked = jnp.concatenate([jnp.where(lane == h, q, zero) for h in range(4)], axis=0)
    scores = lax.dot_general(stacked, k, (((1,), (1,)), ((), ())), preferred_element_type=F32)
    if mask is not None:
        scores = jnp.where(mask, scores, -1e30)
    e = jnp.exp(scores - jnp.max(scores, axis=1, keepdims=True))
    total = jnp.sum(e, axis=1, keepdims=True)
    mixed = mm(e.astype(BF16), v) * (1.0 / total)
    out = mixed[0:count]
    for h in range(1, 4):
        out = jnp.where(lane == h, mixed[h * count : (h + 1) * count], out)
    return out


def middle_rows(stream, attended, wo):
    return round_bf16(stream + mm(attended, wo[...]))


def finish_rows(stream, attended, wo, wu, wd, gain):
    return feed_rows(middle_rows(stream, attended, wo), wu, wd, gain)


def feed_rows(middle, wu, wd, gain):
    hidden_in = norm_rows(middle, gain).astype(BF16)
    total = middle
    for c in range(4):
        raised = mm(hidden_in, wu[:, c * 512 : (c + 1) * 512])
        total = total + mm(gelu(raised).astype(BF16), wd[c * 512 : (c + 1) * 512, :])
    return round_bf16(total)


def put_rows(ref, start, values):
    for j in range(4):
        ref[j, start : start + values.shape[0], :] = values[:, j * 128 : (j + 1) * 128]


def window_runs(base, levels, first_half):
    if first_half is None:
        return [(base + level, 72) for level in levels]
    return [(base + half * 144 + level, 36) for half in (first_half, 1 - first_half) for level in levels]


def gather_run(src, j, runs):
    return jnp.concatenate([src[j, pl.ds(start, count, stride=4), :] for start, count in runs], axis=0)


def scatter_run(dst, group, runs, out):
    at = 0
    for start, count in runs:
        for j in range(2):
            dst[group * 2 + j, pl.ds(start, count, stride=4), :] = out[at : at + count, j * 128 : (j + 1) * 128]
        at += count


def gather_windows(src, dst, windows):
    for w, runs in enumerate(windows):
        for j in range(4):
            dst[w * WIN : (w + 1) * WIN, j * 128 : (j + 1) * 128] = gather_run(src, j, runs).astype(BF16)


def project(nw, packed, wqkv):
    for c in range(6):
        packed[:, c * 256 : (c + 1) * 256] = mm(nw[...], wqkv[:, c * 256 : (c + 1) * 256]).astype(BF16)


def half_of(ref, which):
    pieces = [ref[j, 0:ALL, :].reshape(ROWS, 48, 128)[:, which * 24 : which * 24 + 24].reshape(HALF, 128) for j in range(4)]
    return jnp.concatenate(pieces, axis=1)


def load(sems, *pairs):
    groups, used = [], 0
    for source, target in pairs:
        rows = target.shape[0]
        parts = 4 if rows >= 512 else 1
        step = rows // parts
        group = []
        for i in range(parts):
            piece = (source.at[pl.ds(i * step, step)], target.at[pl.ds(i * step, step)]) if parts > 1 else (source, target)
            group.append(pltpu.make_async_copy(*piece, sems.at[used]))
            group[-1].start()
            used += 1
        groups.append(group)
    return groups


def wait(*groups):
    for group in groups:
        for copy in group:
            copy.wait()


def lanes(ref):
    return jnp.concatenate([ref[j] for j in range(4)], axis=1)


def take_stream(x, dst, at, rows, copies=None):
    for p in range(6):
        if copies is not None:
            wait(copies[p])
        for r in range(rows):
            pair = jnp.concatenate([x[2 * p, r].astype(F32), x[2 * p + 1, r].astype(F32)], axis=0)
            put_rows(dst, at + r * 48 + p * 8, pair)


PLAIN = [window_runs(i * 288, levels, None) for levels in ((0, 1), (2, 3)) for i in range(3)]


def first_kernel(x_h, wqkv_h, wo_h, wu_h, wd_h, gains_h, first_a, normed_a, middle_b, wqkv, wo, wu, wd, gains,
                 x, xs, ns, nw, packed, sems):
    pairs = [(x_h.at[pl.ds(2 * p, 2)], x.at[pl.ds(2 * p, 2)]) for p in range(6)]
    early = load(sems, *pairs, (gains_h, gains), (wqkv_h.at[0], wqkv))
    take_stream(x, xs, 0, ROWS, early)
    wait(early[6])
    put_rows(ns, 0, norm_rows(lanes(xs), gains[0, 0:1]))
    gather_windows(ns, nw, PLAIN)
    wait(early[7])
    copies = load(sems.at[11:], (wo_h.at[0], wo), (wu_h.at[0], wu), (wd_h.at[0], wd))
    project(nw, packed, wqkv)
    for w, runs in enumerate(PLAIN):
        for group in range(2):
            scatter_run(ns, group, runs, attend_unit(packed, w * WIN, WIN, group, None))
    wait(*copies)
    middle_b[...] = middle_rows(half_of(xs, 1), half_of(ns, 1).astype(BF16), wo).astype(BF16)
    result = finish_rows(half_of(xs, 0), half_of(ns, 0).astype(BF16), wo, wu, wd, gains[0, 1:2])
    first_a[...] = result.astype(BF16)
    normed_a[...] = norm_rows(result, gains[1, 0:1]).astype(BF16)


BESIDE = [window_runs(side * 288, levels, 1 - side) for levels in ((0, 1), (2, 3)) for side in range(2)]


def halo_kernel(before, after, wqkv, wo, wu, wd, gains, halo_a, halo_b, xs, ns, nw, packed):
    take_stream(before, xs, 0, 6)
    take_stream(after, xs, 288, 6)
    put_rows(ns, 0, norm_rows(lanes(xs), gains[0, 0:1]))
    gather_windows(ns, nw, BESIDE)
    project(nw, packed, wqkv)
    attended, stream = [], []
    for w, runs in enumerate(BESIDE):
        parts = [attend_unit(packed, w * WIN, 72, group, None) for group in range(2)]
        attended.append(jnp.concatenate(parts, axis=1))
        stream.append(jnp.concatenate([gather_run(xs, j, runs[:2]) for j in range(4)], axis=1))
    result = finish_rows(jnp.concatenate(stream, axis=0), jnp.concatenate(attended, axis=0).astype(BF16),
                         wo, wu, wd, gains[0, 1:2])
    result = norm_rows(result, gains[1, 0:1])
    for w, runs in enumerate(BESIDE):
        for group in range(2):
            scatter_run(ns, group, runs[:2], result[w * 72 : w * 72 + 72, group * 256 : group * 256 + 256])
    near = jnp.concatenate([lanes(ns)[144:288], lanes(ns)[288:432]], axis=0).reshape(6, 48, D)
    halo_a[...] = near[:, 0:24].reshape(144, D).astype(BF16)
    halo_b[...] = near[:, 24:48].reshape(144, D).astype(BF16)


def second_kernel(middle_b, wu, wd, gains, first_b, normed_b):
    result = feed_rows(middle_b[...].astype(F32), wu, wd, gains[0, 1:2])
    first_b[...] = result.astype(BF16)
    normed_b[...] = norm_rows(result, gains[1, 0:1]).astype(BF16)


HALVES = (1, None, None, 0)
SHIFTED = [window_runs(i * 288, levels, HALVES[i]) for levels in ((1, 2), (3, 0)) for i in range(4)]


def third_kernel(edge, n_b, n_ra, halo_b, halo_ra, wqkv_h, wo_h, wu_h, wd_h, z_b, z_ra, wo, wu, wd,
                 ns, nw, packed, wqkv, sems):
    early = load(sems, (wqkv_h.at[1], wqkv))
    for which, (ref, halo) in enumerate(((n_b, halo_b), (n_ra, halo_ra))):
        rows = ref[...].astype(F32).reshape(ROWS, 24, D)
        extra = halo[...].astype(F32).reshape(6, 24, D)
        for r in range(24):
            put_rows(ns, r * 48 + which * 24, rows[r - 3] if 3 <= r < 21 else extra[r if r < 3 else r - 18])
    copies = load(sems.at[4:], (wo_h.at[1], wo), (wu_h.at[1], wu), (wd_h.at[1], wd))
    gather_windows(ns, nw, SHIFTED)
    wait(*early)
    project(nw, packed, wqkv)
    for w, runs in enumerate(SHIFTED):
        i, lonely = w % 4, w >= 4
        count = WIN if HALVES[i] is None else 72
        key = lax.broadcasted_iota(jnp.int32, (4 * count, WIN), 1)
        query = lax.rem(lax.broadcasted_iota(jnp.int32, (4 * count, WIN), 0), count)
        mask = None
        if lonely:
            mask = (lax.rem(key, count) < count // 2) == (query < count // 2)
        if count == 72:
            inside = (key < 72) | (edge[i // 3] == 0)
            mask = inside if mask is None else mask & inside
            runs = runs[:2]
        runs = [(start - 144, length) for start, length in runs]
        for group in range(2):
            scatter_run(ns, group, runs, attend_unit(packed, w * WIN, count, group, mask))
    z_b[...] = half_of(ns, 0).astype(BF16)
    z_ra[...] = half_of(ns, 1).astype(BF16)
    wait(*copies)


def merge_half(values, gain, wm, landed, out):
    pairs = values[: 8 * 48].reshape(4, 2, 2, 3, 8, D)
    last = values[8 * 48 :].reshape(1, 2, 3, 8, D)
    top = lax.broadcasted_iota(jnp.int32, (120, D), 0) % 8 < 4
    parts = []
    for rp in range(2):
        even = jnp.concatenate([pairs[:, 0, rp], last[:, rp]], axis=0).reshape(15, 8, D)
        odd = jnp.concatenate([pairs[:, 1, rp], last[:, rp]], axis=0).reshape(15, 8, D)
        even_turned = pltpu.roll(even, 4, 1).reshape(120, D)
        odd_turned = pltpu.roll(odd, 4, 1).reshape(120, D)
        parts.append(jnp.where(top, even.reshape(120, D), odd_turned))
        parts.append(jnp.where(top, even_turned, odd.reshape(120, D)))
    center = sum(jnp.sum(p, axis=-1, keepdims=True) for p in parts) * (1.0 / 2048)
    parts = [p - center for p in parts]
    spread = sum(jnp.sum(p * p, axis=-1, keepdims=True) for p in parts) * (1.0 / 2048)
    scale = lax.rsqrt(spread + EPSILON)
    total = None
    for i, p in enumerate(parts):
        normed = (p * scale * gain[0:1, i * 512 : (i + 1) * 512]).astype(BF16)
        landed(i)
        term = mm(normed, wm[i * 512 : (i + 1) * 512, :])
        total = term if total is None else total + term
    for j in range(9):
        for i in range(3):
            at = (j // 2 * 3 + i) * 8 + j % 2 * 4
            out[i, j] = total[at : at + 4].astype(BF16)


def fourth_kernel(f_b, att_b, wo, wu, wd, gains, mg_h, wm_h, out_b, gain, wm, sems):
    copies = load(sems, (mg_h, gain), (wm_h, wm))
    second = finish_rows(f_b[...].astype(F32), att_b[...], wo, wu, wd, gains[1, 1:2])
    wait(copies[0])
    merge_half(second, gain, wm, lambda i: copies[1][i].wait(), out_b)


def fifth_kernel(f_a, att_a, out_b, wo, wu, wd, gains, gain, wm, out):
    second = finish_rows(f_a[...].astype(F32), att_a[...], wo, wu, wd, gains[1, 1:2])
    merge_half(second, gain, wm, lambda i: None, out)
    for i in range(3):
        out[3 + i] = out_b[i]


VM = pl.BlockSpec(memory_space=pltpu.VMEM)


def half(count):
    return [pltpu.VMEM((HALF, D), BF16)] * count


def rows_f32(tokens):
    return pltpu.VMEM((4, tokens, 128), F32)


def attention_scratch(tokens):
    return [rows_f32(tokens), pltpu.VMEM((tokens, D), BF16), pltpu.VMEM((tokens, 3 * D), BF16)]


QKV = [pltpu.VMEM((D, 3 * D), BF16)]
FINISH = [pltpu.VMEM((D, D), BF16), pltpu.VMEM((D, FF), BF16), pltpu.VMEM((FF, D), BF16)]
GAINS = [pltpu.VMEM((2, 2, D), F32)]
MERGE = [pltpu.VMEM((1, 4 * D), F32), pltpu.VMEM((4 * D, 1024), BF16)]


def call(kernel, name, outs, args, scratch, sems, flops):
    values = [pltpu.with_memory_space_constraint(v, pltpu.HBM) if m is pltpu.HBM else v for v, m in args]
    outs = [jax.ShapeDtypeStruct(o.shape, o.dtype) for o in outs]
    return pl.pallas_call(
        kernel,
        out_shape=outs,
        in_specs=[pl.BlockSpec(memory_space=m) for _, m in args],
        out_specs=jax.tree.map(lambda _: VM, outs),
        scratch_shapes=scratch + ([pltpu.SemaphoreType.DMA((4 * sems,))] if sems else []),
        compiler_params=pltpu.CompilerParams(vmem_limit_bytes=VMEM_LIMIT),
        cost_estimate=pl.CostEstimate(flops=flops, bytes_accessed=6_000_000, transcendentals=900_000),
        name=name,
    )(*values)


def hbm(*values):
    return [(v, pltpu.HBM) for v in values]


def vmem(*values):
    return [(v, pltpu.VMEM) for v in values]


def ring(value, axis, by):
    length = lax.axis_size(axis)
    return lax.ppermute(value, axis, [(i, (i + by) % length) for i in range(length)])


def body(stream, w_qkv, w_out, w_up, w_down, gains, merge_gain, w_merge):
    place = lax.axis_index("lat")
    edge = jnp.stack([place == 0, place == lax.axis_size("lat") - 1]).astype(jnp.int32)
    after = ring(stream[:, :6], "lat", -1)
    before = ring(stream[:, 12:], "lat", 1)
    first_a, normed_a, middle_b, wqkv0, wo0, wu0, wd0, gains = call(
        first_kernel, "block_one", half(3) + QKV + FINISH + GAINS, hbm(stream, w_qkv, w_out, w_up, w_down, gains),
        [pltpu.VMEM((COLS, ROWS, LEV, D), BF16), rows_f32(ALL)] + attention_scratch(ALL), 8, 6_000_000_000)
    normed_ra = ring(normed_a, "lon", -1)
    halo_a, halo_b = call(
        halo_kernel, "block_one_beside", [pltpu.VMEM((144, D), BF16)] * 2,
        vmem(before, after, wqkv0, wo0, wu0, wd0, gains), [rows_f32(576)] + attention_scratch(576), 0, 4_000_000_000)
    halo_ra = ring(halo_a, "lon", -1)
    first_b, normed_b = call(
        second_kernel, "block_one_rest", half(2), vmem(middle_b, wu0, wd0, gains), [], 0, 4_000_000_000)
    z_b, z_ra, wo1, wu1, wd1 = call(
        third_kernel, "shifted_attention", half(2) + FINISH,
        [(edge, pltpu.SMEM)] + vmem(normed_b, normed_ra, halo_b, halo_ra) + hbm(w_qkv, w_out, w_up, w_down),
        attention_scratch(1152) + QKV, 4, 4_000_000_000)
    att_a = ring(z_ra, "lon", 1)
    out_b, mg, wm = call(
        fourth_kernel, "block_two_rest", [jax.ShapeDtypeStruct((3, 9, LEV, 1024), BF16)] + MERGE,
        vmem(first_b, z_b, wo1, wu1, wd1, gains) + hbm(merge_gain.reshape(1, -1), w_merge), [], 2, 5_000_000_000)
    out, = call(
        fifth_kernel, "merge", [jax.ShapeDtypeStruct((6, 9, LEV, 1024), BF16)],
        vmem(first_a, att_a, out_b, wo1, wu1, wd1, gains, mg, wm), [], 0, 5_000_000_000)
    return out


def solution(mesh):
    return jax.shard_map(
        body,
        mesh=mesh,
        in_specs=(P("lon", "lat", None, None), P(), P(), P(), P(), P(), P(), P()),
        out_specs=P("lon", "lat", None, None),
        check_vma=False,
    )
```

```python
import functools

import jax
import jax.numpy as jnp
from jax import lax
from jax.experimental import pallas as pl
from jax.experimental.pallas import tpu as pltpu
from jax.sharding import PartitionSpec as P

EPSILON = 1e-05
D = 512
FF = 2048
COLS, ROWS, LEV = 12, 18, 4
HALF = 432
ALL = 864
WIN = 144
F32 = jnp.float32
BF16 = jnp.bfloat16
VMEM_LIMIT = 20 * 1024 * 1024


def norm_rows(values, gain):
    center = jnp.mean(values, axis=-1, keepdims=True)
    off = values - center
    spread = jnp.mean(off * off, axis=-1, keepdims=True)
    return off * lax.rsqrt(spread + EPSILON) * gain


def round_bf16(values):
    return values.astype(BF16).astype(F32)


def mm(a, b):
    return jnp.dot(a, b, preferred_element_type=F32)


def gelu(x):
    inner = 0.7978845608028654 * (x + 0.044715 * (x * x * x))
    return 0.5 * x * (1.0 + jnp.tanh(inner))


def attend_unit(packed_ref, row0, count, group, mask):
    span = pl.ds(row0, WIN)
    lo = group * 256
    q = packed_ref[pl.ds(row0, count), lo : lo + 256] * jnp.asarray(0.125, BF16)
    k = packed_ref[span, D + lo : D + lo + 256]
    v = packed_ref[span, 2 * D + lo : 2 * D + lo + 256]
    lane = lax.broadcasted_iota(jnp.int32, (count, 256), 1) // 64
    zero = jnp.zeros_like(q)
    stacked = jnp.concatenate([jnp.where(lane == h, q, zero) for h in range(4)], axis=0)
    scores = lax.dot_general(stacked, k, (((1,), (1,)), ((), ())), preferred_element_type=F32)
    if mask is not None:
        scores = jnp.where(mask, scores, -1e30)
    e = jnp.exp(scores - jnp.max(scores, axis=1, keepdims=True))
    total = jnp.sum(e, axis=1, keepdims=True)
    mixed = mm(e.astype(BF16), v) * (1.0 / total)
    out = mixed[0:count]
    for h in range(1, 4):
        out = jnp.where(lane == h, mixed[h * count : (h + 1) * count], out)
    return out


def middle_rows(stream, attended, wo):
    return round_bf16(stream + mm(attended, wo[...]))


def finish_rows(stream, attended, wo, wu, wd, gain):
    return feed_rows(middle_rows(stream, attended, wo), wu, wd, gain)


def feed_rows(middle, wu, wd, gain):
    hidden_in = norm_rows(middle, gain).astype(BF16)
    total = middle
    for c in range(4):
        raised = mm(hidden_in, wu[:, c * 512 : (c + 1) * 512])
        total = total + mm(gelu(raised).astype(BF16), wd[c * 512 : (c + 1) * 512, :])
    return round_bf16(total)


def put_rows(ref, start, values):
    for j in range(4):
        ref[j, start : start + values.shape[0], :] = values[:, j * 128 : (j + 1) * 128]


def window_runs(base, levels, first_half):
    if first_half is None:
        return [(base + level, 72) for level in levels]
    return [(base + half * 144 + level, 36) for half in (first_half, 1 - first_half) for level in levels]


def gather_run(src, j, runs):
    return jnp.concatenate([src[j, pl.ds(start, count, stride=4), :] for start, count in runs], axis=0)


def scatter_run(dst, group, runs, out):
    at = 0
    for start, count in runs:
        for j in range(2):
            dst[group * 2 + j, pl.ds(start, count, stride=4), :] = out[at : at + count, j * 128 : (j + 1) * 128]
        at += count


def gather_windows(src, dst, windows):
    for w, runs in enumerate(windows):
        for j in range(4):
            dst[w * WIN : (w + 1) * WIN, j * 128 : (j + 1) * 128] = gather_run(src, j, runs).astype(BF16)


def project(nw, packed, wqkv):
    for c in range(6):
        packed[:, c * 256 : (c + 1) * 256] = mm(nw[...], wqkv[:, c * 256 : (c + 1) * 256]).astype(BF16)


def half_of(ref, which):
    pieces = [ref[j, 0:ALL, :].reshape(ROWS, 48, 128)[:, which * 24 : which * 24 + 24].reshape(HALF, 128) for j in range(4)]
    return jnp.concatenate(pieces, axis=1)


def load(sems, *pairs):
    groups, used = [], 0
    for source, target in pairs:
        rows = target.shape[0]
        parts = 4 if rows >= 512 else 1
        step = rows // parts
        group = []
        for i in range(parts):
            piece = (source.at[pl.ds(i * step, step)], target.at[pl.ds(i * step, step)]) if parts > 1 else (source, target)
            group.append(pltpu.make_async_copy(*piece, sems.at[used]))
            group[-1].start()
            used += 1
        groups.append(group)
    return groups


def wait(*groups):
    for group in groups:
        for copy in group:
            copy.wait()


def lanes(ref, rows):
    return jnp.concatenate([ref[j, 0:rows, :] for j in range(4)], axis=1)


def take_stream(x, dst, at, rows, copies=None):
    for p in range(6):
        if copies is not None:
            wait(copies[p])
        for r in range(rows):
            pair = jnp.concatenate([x[2 * p, r].astype(F32), x[2 * p + 1, r].astype(F32)], axis=0)
            put_rows(dst, at + r * 48 + p * 8, pair)


PLAIN = [window_runs(i * 288, levels, None) for levels in ((0, 1), (2, 3)) for i in range(3)]


def first_kernel(x_h, wqkv_h, wo_h, wu_h, wd_h, gains_h, first_a, normed_a, middle_b, wqkv, wo, wu, wd, gains,
                 x, xs, ns, nw, packed, sems):
    pairs = [(x_h.at[pl.ds(2 * p, 2)], x.at[pl.ds(2 * p, 2)]) for p in range(6)]
    early = load(sems, *pairs, (gains_h, gains), (wqkv_h.at[0], wqkv))
    take_stream(x, xs, 0, ROWS, early)
    wait(early[6])
    put_rows(ns, 0, norm_rows(lanes(xs, ALL), gains[0, 0:1]))
    gather_windows(ns, nw, PLAIN)
    wait(early[7])
    copies = load(sems.at[11:], (wo_h.at[0], wo), (wu_h.at[0], wu), (wd_h.at[0], wd))
    project(nw, packed, wqkv)
    for w, runs in enumerate(PLAIN):
        for group in range(2):
            scatter_run(ns, group, runs, attend_unit(packed, w * WIN, WIN, group, None))
    wait(*copies)
    middle_b[...] = middle_rows(half_of(xs, 1), half_of(ns, 1).astype(BF16), wo).astype(BF16)
    result = finish_rows(half_of(xs, 0), half_of(ns, 0).astype(BF16), wo, wu, wd, gains[0, 1:2])
    first_a[...] = result.astype(BF16)
    normed_a[...] = norm_rows(result, gains[1, 0:1]).astype(BF16)


BESIDE = [window_runs(side * 288, levels, 1 - side) for levels in ((0, 1), (2, 3)) for side in range(2)]


def halo_kernel(before, after, wqkv, wo, wu, wd, gains, halo_a, halo_b, xs, ns, nw, packed):
    take_stream(before, xs, 0, 6)
    take_stream(after, xs, 288, 6)
    put_rows(ns, 0, norm_rows(lanes(xs, 576), gains[0, 0:1]))
    gather_windows(ns, nw, BESIDE)
    project(nw, packed, wqkv)
    attended, stream = [], []
    for w, runs in enumerate(BESIDE):
        parts = [attend_unit(packed, w * WIN, 72, group, None) for group in range(2)]
        attended.append(jnp.concatenate(parts, axis=1))
        stream.append(jnp.concatenate([gather_run(xs, j, runs[:2]) for j in range(4)], axis=1))
    result = finish_rows(jnp.concatenate(stream, axis=0), jnp.concatenate(attended, axis=0).astype(BF16),
                         wo, wu, wd, gains[0, 1:2])
    result = norm_rows(result, gains[1, 0:1])
    for w, runs in enumerate(BESIDE):
        for group in range(2):
            scatter_run(ns, group, runs[:2], result[w * 72 : w * 72 + 72, group * 256 : group * 256 + 256])
    near = lanes(ns, 432)[144:].reshape(6, 48, D)
    halo_a[...] = near[:, 0:24].reshape(144, D).astype(BF16)
    halo_b[...] = near[:, 24:48].reshape(144, D).astype(BF16)


def second_kernel(middle_b, wu, wd, gains, first_b, normed_b):
    result = feed_rows(middle_b[...].astype(F32), wu, wd, gains[0, 1:2])
    first_b[...] = result.astype(BF16)
    normed_b[...] = norm_rows(result, gains[1, 0:1]).astype(BF16)


HALVES = (1, None, None, 0)
SHIFTED = [window_runs(i * 288, levels, HALVES[i]) for levels in ((1, 2), (3, 0)) for i in range(4)]


def third_kernel(edge, n_b, n_ra, halo_b, halo_ra, wqkv_h, wo_h, wu_h, wd_h, z_b, z_ra, wo, wu, wd,
                 ns, nw, packed, wqkv, sems):
    early = load(sems, (wqkv_h.at[1], wqkv))
    for which, (ref, halo) in enumerate(((n_b, halo_b), (n_ra, halo_ra))):
        rows = ref[...].astype(F32).reshape(ROWS, 24, D)
        extra = halo[...].astype(F32).reshape(6, 24, D)
        for r in range(24):
            put_rows(ns, r * 48 + which * 24, rows[r - 3] if 3 <= r < 21 else extra[r if r < 3 else r - 18])
    copies = load(sems.at[4:], (wo_h.at[1], wo), (wu_h.at[1], wu), (wd_h.at[1], wd))
    gather_windows(ns, nw, SHIFTED)
    wait(*early)
    project(nw, packed, wqkv)
    for w, runs in enumerate(SHIFTED):
        i, lonely = w % 4, w >= 4
        count = WIN if HALVES[i] is None else 72
        key = lax.broadcasted_iota(jnp.int32, (4 * count, WIN), 1)
        query = lax.rem(lax.broadcasted_iota(jnp.int32, (4 * count, WIN), 0), count)
        mask = None
        if lonely:
            mask = (lax.rem(key, count) < count // 2) == (query < count // 2)
        if count == 72:
            inside = (key < 72) | (edge[i // 3] == 0)
            mask = inside if mask is None else mask & inside
            runs = runs[:2]
        runs = [(start - 144, length) for start, length in runs]
        for group in range(2):
            scatter_run(ns, group, runs, attend_unit(packed, w * WIN, count, group, mask))
    z_b[...] = half_of(ns, 0).astype(BF16)
    z_ra[...] = half_of(ns, 1).astype(BF16)
    wait(*copies)


def merge_half(values, gain, wm, landed, out):
    pairs = values[: 8 * 48].reshape(4, 2, 2, 3, 8, D)
    last = values[8 * 48 :].reshape(1, 2, 3, 8, D)
    top = lax.broadcasted_iota(jnp.int32, (120, D), 0) % 8 < 4
    parts = []
    for rp in range(2):
        even = jnp.concatenate([pairs[:, 0, rp], last[:, rp]], axis=0).reshape(15, 8, D)
        odd = jnp.concatenate([pairs[:, 1, rp], last[:, rp]], axis=0).reshape(15, 8, D)
        even_turned = pltpu.roll(even, 4, 1).reshape(120, D)
        odd_turned = pltpu.roll(odd, 4, 1).reshape(120, D)
        parts.append(jnp.where(top, even.reshape(120, D), odd_turned))
        parts.append(jnp.where(top, even_turned, odd.reshape(120, D)))
    center = sum(jnp.sum(p, axis=-1, keepdims=True) for p in parts) * (1.0 / 2048)
    parts = [p - center for p in parts]
    spread = sum(jnp.sum(p * p, axis=-1, keepdims=True) for p in parts) * (1.0 / 2048)
    scale = lax.rsqrt(spread + EPSILON)
    total = None
    for i, p in enumerate(parts):
        normed = (p * scale * gain[0:1, i * 512 : (i + 1) * 512]).astype(BF16)
        landed(i)
        term = mm(normed, wm[i * 512 : (i + 1) * 512, :])
        total = term if total is None else total + term
    for j in range(9):
        for i in range(3):
            at = (j // 2 * 3 + i) * 8 + j % 2 * 4
            out[i, j] = total[at : at + 4].astype(BF16)


def fourth_kernel(f_b, att_b, wo, wu, wd, gains, mg_h, wm_h, out_b, gain, wm, sems):
    copies = load(sems, (mg_h, gain), (wm_h, wm))
    second = finish_rows(f_b[...].astype(F32), att_b[...], wo, wu, wd, gains[1, 1:2])
    wait(copies[0])
    merge_half(second, gain, wm, lambda i: copies[1][i].wait(), out_b)


def fifth_kernel(f_a, att_a, out_b, wo, wu, wd, gains, gain, wm, out):
    second = finish_rows(f_a[...].astype(F32), att_a[...], wo, wu, wd, gains[1, 1:2])
    merge_half(second, gain, wm, lambda i: None, out)
    for i in range(3):
        out[3 + i] = out_b[i]


VM = pl.BlockSpec(memory_space=pltpu.VMEM)


def half(count):
    return [pltpu.VMEM((HALF, D), BF16)] * count


def rows_f32(tokens):
    return pltpu.VMEM((4, tokens + 32, 128), F32)


def attention_scratch(tokens):
    return [rows_f32(tokens), pltpu.VMEM((tokens, D), BF16), pltpu.VMEM((tokens, 3 * D), BF16)]


QKV = [pltpu.VMEM((D, 3 * D), BF16)]
FINISH = [pltpu.VMEM((D, D), BF16), pltpu.VMEM((D, FF), BF16), pltpu.VMEM((FF, D), BF16)]
GAINS = [pltpu.VMEM((2, 2, D), F32)]
MERGE = [pltpu.VMEM((1, 4 * D), F32), pltpu.VMEM((4 * D, 1024), BF16)]


def call(kernel, name, outs, args, scratch, sems, flops):
    values = [pltpu.with_memory_space_constraint(v, pltpu.HBM) if m is pltpu.HBM else v for v, m in args]
    outs = [jax.ShapeDtypeStruct(o.shape, o.dtype) for o in outs]
    return pl.pallas_call(
        kernel,
        out_shape=outs,
        in_specs=[pl.BlockSpec(memory_space=m) for _, m in args],
        out_specs=jax.tree.map(lambda _: VM, outs),
        scratch_shapes=scratch + ([pltpu.SemaphoreType.DMA((4 * sems,))] if sems else []),
        compiler_params=pltpu.CompilerParams(vmem_limit_bytes=VMEM_LIMIT),
        cost_estimate=pl.CostEstimate(flops=flops, bytes_accessed=6_000_000, transcendentals=900_000),
        name=name,
    )(*values)


def hbm(*values):
    return [(v, pltpu.HBM) for v in values]


def vmem(*values):
    return [(v, pltpu.VMEM) for v in values]


def ring(value, axis, by):
    length = lax.axis_size(axis)
    return lax.ppermute(value, axis, [(i, (i + by) % length) for i in range(length)])


def body(stream, w_qkv, w_out, w_up, w_down, gains, merge_gain, w_merge):
    place = lax.axis_index("lat")
    edge = jnp.stack([place == 0, place == lax.axis_size("lat") - 1]).astype(jnp.int32)
    after = ring(stream[:, :6], "lat", -1)
    before = ring(stream[:, 12:], "lat", 1)
    first_a, normed_a, middle_b, wqkv0, wo0, wu0, wd0, gains = call(
        first_kernel, "block_one", half(3) + QKV + FINISH + GAINS, hbm(stream, w_qkv, w_out, w_up, w_down, gains),
        [pltpu.VMEM((COLS, ROWS, LEV, D), BF16), rows_f32(ALL)] + attention_scratch(ALL), 8, 6_000_000_000)
    normed_ra = ring(normed_a, "lon", -1)
    halo_a, halo_b = call(
        halo_kernel, "block_one_beside", [pltpu.VMEM((144, D), BF16)] * 2,
        vmem(before, after, wqkv0, wo0, wu0, wd0, gains), [rows_f32(576)] + attention_scratch(576), 0, 4_000_000_000)
    halo_ra = ring(halo_a, "lon", -1)
    first_b, normed_b = call(
        second_kernel, "block_one_rest", half(2), vmem(middle_b, wu0, wd0, gains), [], 0, 4_000_000_000)
    z_b, z_ra, wo1, wu1, wd1 = call(
        third_kernel, "shifted_attention", half(2) + FINISH,
        [(edge, pltpu.SMEM)] + vmem(normed_b, normed_ra, halo_b, halo_ra) + hbm(w_qkv, w_out, w_up, w_down),
        attention_scratch(1152) + QKV, 4, 4_000_000_000)
    att_a = ring(z_ra, "lon", 1)
    out_b, mg, wm = call(
        fourth_kernel, "block_two_rest", [jax.ShapeDtypeStruct((3, 9, LEV, 1024), BF16)] + MERGE,
        vmem(first_b, z_b, wo1, wu1, wd1, gains) + hbm(merge_gain.reshape(1, -1), w_merge), [], 2, 5_000_000_000)
    out, = call(
        fifth_kernel, "merge", [jax.ShapeDtypeStruct((6, 9, LEV, 1024), BF16)],
        vmem(first_a, att_a, out_b, wo1, wu1, wd1, gains, mg, wm), [], 0, 5_000_000_000)
    return out


def solution(mesh):
    return jax.shard_map(
        body,
        mesh=mesh,
        in_specs=(P("lon", "lat", None, None), P(), P(), P(), P(), P(), P(), P()),
        out_specs=P("lon", "lat", None, None),
        check_vma=False,
    )
```

```python
import functools

import jax
import jax.numpy as jnp
from jax import lax
from jax.experimental import pallas as pl
from jax.experimental.pallas import tpu as pltpu
from jax.sharding import PartitionSpec as P

EPSILON = 1e-05
D = 512
FF = 2048
COLS, ROWS, LEV = 12, 18, 4
HALF = 432
ALL = 864
WIN = 144
F32 = jnp.float32
BF16 = jnp.bfloat16
VMEM_LIMIT = 20 * 1024 * 1024


def norm_rows(values, gain):
    center = jnp.mean(values, axis=-1, keepdims=True)
    off = values - center
    spread = jnp.mean(off * off, axis=-1, keepdims=True)
    return off * lax.rsqrt(spread + EPSILON) * gain


def round_bf16(values):
    return values.astype(BF16).astype(F32)


def mm(a, b):
    return jnp.dot(a, b, preferred_element_type=F32)


def gelu(x):
    half = 0.5 * x
    return half + half * jnp.tanh(x * (0.7978845608028654 + 0.035677408136300125 * (x * x)))


def attend_unit(packed_ref, row0, count, group, mask):
    span = pl.ds(row0, WIN)
    lo = group * 256
    q = packed_ref[pl.ds(row0, count), lo : lo + 256] * jnp.asarray(0.125, BF16)
    k = packed_ref[span, D + lo : D + lo + 256]
    v = packed_ref[span, 2 * D + lo : 2 * D + lo + 256]
    lane = lax.broadcasted_iota(jnp.int32, (count, 256), 1) // 64
    zero = jnp.zeros_like(q)
    stacked = jnp.concatenate([jnp.where(lane == h, q, zero) for h in range(4)], axis=0)
    scores = lax.dot_general(stacked, k, (((1,), (1,)), ((), ())), preferred_element_type=F32)
    if mask is not None:
        scores = jnp.where(mask, scores, -1e30)
    e = jnp.exp(scores - jnp.max(scores, axis=1, keepdims=True))
    total = jnp.sum(e, axis=1, keepdims=True)
    mixed = mm(e.astype(BF16), v) * (1.0 / total)
    out = mixed[0:count]
    for h in range(1, 4):
        out = jnp.where(lane == h, mixed[h * count : (h + 1) * count], out)
    return out


def middle_rows(stream, attended, wo):
    return round_bf16(stream + mm(attended, wo[...]))


def finish_rows(stream, attended, wo, wu, wd, gain):
    return feed_rows(middle_rows(stream, attended, wo), wu, wd, gain)


def feed_rows(middle, wu, wd, gain):
    hidden_in = norm_rows(middle, gain).astype(BF16)
    total = middle
    for c in range(4):
        raised = mm(hidden_in, wu[:, c * 512 : (c + 1) * 512])
        total = total + mm(gelu(raised).astype(BF16), wd[c * 512 : (c + 1) * 512, :])
    return round_bf16(total)


def put_rows(ref, start, values):
    for j in range(4):
        ref[j, start : start + values.shape[0], :] = values[:, j * 128 : (j + 1) * 128]


def window_runs(base, levels, first_half):
    if first_half is None:
        return [(base + level, 72) for level in levels]
    return [(base + half * 144 + level, 36) for half in (first_half, 1 - first_half) for level in levels]


def gather_run(src, j, runs):
    return jnp.concatenate([src[j, pl.ds(start, count, stride=4), :] for start, count in runs], axis=0)


def scatter_run(dst, group, runs, out):
    at = 0
    for start, count in runs:
        for j in range(2):
            dst[group * 2 + j, pl.ds(start, count, stride=4), :] = out[at : at + count, j * 128 : (j + 1) * 128]
        at += count


def gather_windows(src, dst, windows):
    for w, runs in enumerate(windows):
        for j in range(4):
            dst[w * WIN : (w + 1) * WIN, j * 128 : (j + 1) * 128] = gather_run(src, j, runs).astype(BF16)


def project(nw, packed, wqkv):
    for c in range(6):
        packed[:, c * 256 : (c + 1) * 256] = mm(nw[...], wqkv[:, c * 256 : (c + 1) * 256]).astype(BF16)


def half_of(ref, which):
    pieces = [ref[j, 0:ALL, :].reshape(ROWS, 48, 128)[:, which * 24 : which * 24 + 24].reshape(HALF, 128) for j in range(4)]
    return jnp.concatenate(pieces, axis=1)


def load(sems, *pairs):
    groups, used = [], 0
    for source, target in pairs:
        rows = target.shape[0]
        parts = 4 if rows >= 512 else 1
        step = rows // parts
        group = []
        for i in range(parts):
            piece = (source.at[pl.ds(i * step, step)], target.at[pl.ds(i * step, step)]) if parts > 1 else (source, target)
            group.append(pltpu.make_async_copy(*piece, sems.at[used]))
            group[-1].start()
            used += 1
        groups.append(group)
    return groups


def wait(*groups):
    for group in groups:
        for copy in group:
            copy.wait()


def lanes(ref, rows):
    return jnp.concatenate([ref[j, 0:rows, :] for j in range(4)], axis=1)


def take_stream(x, dst, at, rows, copies=None):
    for p in range(6):
        if copies is not None:
            wait(copies[p])
        for r in range(rows):
            pair = jnp.concatenate([x[2 * p, r].astype(F32), x[2 * p + 1, r].astype(F32)], axis=0)
            put_rows(dst, at + r * 48 + p * 8, pair)


PLAIN = [window_runs(i * 288, levels, None) for levels in ((0, 1), (2, 3)) for i in range(3)]


def first_kernel(x_h, wqkv_h, wo_h, wu_h, wd_h, gains_h, first_a, normed_a, middle_b, wqkv, wo, wu, wd, gains,
                 x, xs, ns, nw, packed, sems):
    pairs = [(x_h.at[pl.ds(2 * p, 2)], x.at[pl.ds(2 * p, 2)]) for p in range(6)]
    early = load(sems, *pairs, (gains_h, gains), (wqkv_h.at[0], wqkv))
    take_stream(x, xs, 0, ROWS, early)
    wait(early[6])
    put_rows(ns, 0, norm_rows(lanes(xs, ALL), gains[0, 0:1]))
    gather_windows(ns, nw, PLAIN)
    wait(early[7])
    copies = load(sems.at[11:], (wo_h.at[0], wo), (wu_h.at[0], wu), (wd_h.at[0], wd))
    project(nw, packed, wqkv)
    for w, runs in enumerate(PLAIN):
        for group in range(2):
            scatter_run(ns, group, runs, attend_unit(packed, w * WIN, WIN, group, None))
    wait(*copies)
    middle_b[...] = middle_rows(half_of(xs, 1), half_of(ns, 1).astype(BF16), wo).astype(BF16)
    result = finish_rows(half_of(xs, 0), half_of(ns, 0).astype(BF16), wo, wu, wd, gains[0, 1:2])
    first_a[...] = result.astype(BF16)
    normed_a[...] = norm_rows(result, gains[1, 0:1]).astype(BF16)


BESIDE = [window_runs(side * 288, levels, 1 - side) for levels in ((0, 1), (2, 3)) for side in range(2)]


def halo_kernel(before, after, wqkv, wo, wu, wd, gains, halo_a, halo_b, xs, ns, nw, packed):
    take_stream(before, xs, 0, 6)
    take_stream(after, xs, 288, 6)
    put_rows(ns, 0, norm_rows(lanes(xs, 576), gains[0, 0:1]))
    gather_windows(ns, nw, BESIDE)
    project(nw, packed, wqkv)
    attended, stream = [], []
    for w, runs in enumerate(BESIDE):
        parts = [attend_unit(packed, w * WIN, 72, group, None) for group in range(2)]
        attended.append(jnp.concatenate(parts, axis=1))
        stream.append(jnp.concatenate([gather_run(xs, j, runs[:2]) for j in range(4)], axis=1))
    result = finish_rows(jnp.concatenate(stream, axis=0), jnp.concatenate(attended, axis=0).astype(BF16),
                         wo, wu, wd, gains[0, 1:2])
    result = norm_rows(result, gains[1, 0:1])
    for w, runs in enumerate(BESIDE):
        for group in range(2):
            scatter_run(ns, group, runs[:2], result[w * 72 : w * 72 + 72, group * 256 : group * 256 + 256])
    near = lanes(ns, 432)[144:].reshape(6, 48, D)
    halo_a[...] = near[:, 0:24].reshape(144, D).astype(BF16)
    halo_b[...] = near[:, 24:48].reshape(144, D).astype(BF16)


def second_kernel(middle_b, wu, wd, gains, first_b, normed_b):
    result = feed_rows(middle_b[...].astype(F32), wu, wd, gains[0, 1:2])
    first_b[...] = result.astype(BF16)
    normed_b[...] = norm_rows(result, gains[1, 0:1]).astype(BF16)


HALVES = (1, None, None, 0)
SHIFTED = [window_runs(i * 288, levels, HALVES[i]) for levels in ((1, 2), (3, 0)) for i in range(4)]


def third_kernel(edge, n_b, n_ra, halo_b, halo_ra, wqkv_h, wo_h, wu_h, wd_h, z_b, z_ra, wo, wu, wd,
                 ns, nw, packed, wqkv, sems):
    early = load(sems, (wqkv_h.at[1], wqkv))
    for which, (ref, halo) in enumerate(((n_b, halo_b), (n_ra, halo_ra))):
        rows = ref[...].astype(F32).reshape(ROWS, 24, D)
        extra = halo[...].astype(F32).reshape(6, 24, D)
        for r in range(24):
            put_rows(ns, r * 48 + which * 24, rows[r - 3] if 3 <= r < 21 else extra[r if r < 3 else r - 18])
    copies = load(sems.at[4:], (wo_h.at[1], wo), (wu_h.at[1], wu), (wd_h.at[1], wd))
    gather_windows(ns, nw, SHIFTED)
    wait(*early)
    project(nw, packed, wqkv)
    for w, runs in enumerate(SHIFTED):
        i, lonely = w % 4, w >= 4
        count = WIN if HALVES[i] is None else 72
        key = lax.broadcasted_iota(jnp.int32, (4 * count, WIN), 1)
        query = lax.rem(lax.broadcasted_iota(jnp.int32, (4 * count, WIN), 0), count)
        mask = None
        if lonely:
            mask = (lax.rem(key, count) < count // 2) == (query < count // 2)
        if count == 72:
            inside = (key < 72) | (edge[i // 3] == 0)
            mask = inside if mask is None else mask & inside
            runs = runs[:2]
        runs = [(start - 144, length) for start, length in runs]
        for group in range(2):
            scatter_run(ns, group, runs, attend_unit(packed, w * WIN, count, group, mask))
    z_b[...] = half_of(ns, 0).astype(BF16)
    z_ra[...] = half_of(ns, 1).astype(BF16)
    wait(*copies)


def merge_half(values, gain, wm, landed, out):
    pairs = values[: 8 * 48].reshape(4, 2, 2, 3, 8, D)
    last = values[8 * 48 :].reshape(1, 2, 3, 8, D)
    top = lax.broadcasted_iota(jnp.int32, (120, D), 0) % 8 < 4
    parts = []
    for rp in range(2):
        even = jnp.concatenate([pairs[:, 0, rp], last[:, rp]], axis=0).reshape(15, 8, D)
        odd = jnp.concatenate([pairs[:, 1, rp], last[:, rp]], axis=0).reshape(15, 8, D)
        even_turned = pltpu.roll(even, 4, 1).reshape(120, D)
        odd_turned = pltpu.roll(odd, 4, 1).reshape(120, D)
        parts.append(jnp.where(top, even.reshape(120, D), odd_turned))
        parts.append(jnp.where(top, even_turned, odd.reshape(120, D)))
    center = sum(jnp.sum(p, axis=-1, keepdims=True) for p in parts) * (1.0 / 2048)
    parts = [p - center for p in parts]
    spread = sum(jnp.sum(p * p, axis=-1, keepdims=True) for p in parts) * (1.0 / 2048)
    scale = lax.rsqrt(spread + EPSILON)
    total = None
    for i, p in enumerate(parts):
        normed = (p * scale * gain[0:1, i * 512 : (i + 1) * 512]).astype(BF16)
        landed(i)
        term = mm(normed, wm[i * 512 : (i + 1) * 512, :])
        total = term if total is None else total + term
    for j in range(9):
        for i in range(3):
            at = (j // 2 * 3 + i) * 8 + j % 2 * 4
            out[i, j] = total[at : at + 4].astype(BF16)


def fourth_kernel(f_b, att_b, wo, wu, wd, gains, mg_h, wm_h, out_b, gain, wm, sems):
    copies = load(sems, (mg_h, gain), (wm_h, wm))
    second = finish_rows(f_b[...].astype(F32), att_b[...], wo, wu, wd, gains[1, 1:2])
    wait(copies[0])
    merge_half(second, gain, wm, lambda i: copies[1][i].wait(), out_b)


def fifth_kernel(f_a, att_a, out_b, wo, wu, wd, gains, gain, wm, out):
    second = finish_rows(f_a[...].astype(F32), att_a[...], wo, wu, wd, gains[1, 1:2])
    merge_half(second, gain, wm, lambda i: None, out)
    for i in range(3):
        out[3 + i] = out_b[i]


VM = pl.BlockSpec(memory_space=pltpu.VMEM)


def half(count):
    return [pltpu.VMEM((HALF, D), BF16)] * count


def rows_f32(tokens):
    return pltpu.VMEM((4, tokens + 32, 128), F32)


def attention_scratch(tokens):
    return [rows_f32(tokens), pltpu.VMEM((tokens, D), BF16), pltpu.VMEM((tokens, 3 * D), BF16)]


QKV = [pltpu.VMEM((D, 3 * D), BF16)]
FINISH = [pltpu.VMEM((D, D), BF16), pltpu.VMEM((D, FF), BF16), pltpu.VMEM((FF, D), BF16)]
GAINS = [pltpu.VMEM((2, 2, D), F32)]
MERGE = [pltpu.VMEM((1, 4 * D), F32), pltpu.VMEM((4 * D, 1024), BF16)]


def call(kernel, name, outs, args, scratch, sems, flops):
    values = [pltpu.with_memory_space_constraint(v, pltpu.HBM) if m is pltpu.HBM else v for v, m in args]
    outs = [jax.ShapeDtypeStruct(o.shape, o.dtype) for o in outs]
    return pl.pallas_call(
        kernel,
        out_shape=outs,
        in_specs=[pl.BlockSpec(memory_space=m) for _, m in args],
        out_specs=jax.tree.map(lambda _: VM, outs),
        scratch_shapes=scratch + ([pltpu.SemaphoreType.DMA((4 * sems,))] if sems else []),
        compiler_params=pltpu.CompilerParams(vmem_limit_bytes=VMEM_LIMIT),
        cost_estimate=pl.CostEstimate(flops=flops, bytes_accessed=6_000_000, transcendentals=900_000),
        name=name,
    )(*values)


def hbm(*values):
    return [(v, pltpu.HBM) for v in values]


def vmem(*values):
    return [(v, pltpu.VMEM) for v in values]


def ring(value, axis, by):
    length = lax.axis_size(axis)
    return lax.ppermute(value, axis, [(i, (i + by) % length) for i in range(length)])


def body(stream, w_qkv, w_out, w_up, w_down, gains, merge_gain, w_merge):
    place = lax.axis_index("lat")
    edge = jnp.stack([place == 0, place == lax.axis_size("lat") - 1]).astype(jnp.int32)
    after = ring(stream[:, :6], "lat", -1)
    before = ring(stream[:, 12:], "lat", 1)
    first_a, normed_a, middle_b, wqkv0, wo0, wu0, wd0, gains = call(
        first_kernel, "block_one", half(3) + QKV + FINISH + GAINS, hbm(stream, w_qkv, w_out, w_up, w_down, gains),
        [pltpu.VMEM((COLS, ROWS, LEV, D), BF16), rows_f32(ALL)] + attention_scratch(ALL), 8, 6_000_000_000)
    normed_ra = ring(normed_a, "lon", -1)
    halo_a, halo_b = call(
        halo_kernel, "block_one_beside", [pltpu.VMEM((144, D), BF16)] * 2,
        vmem(before, after, wqkv0, wo0, wu0, wd0, gains), [rows_f32(576)] + attention_scratch(576), 0, 4_000_000_000)
    halo_ra = ring(halo_a, "lon", -1)
    first_b, normed_b = call(
        second_kernel, "block_one_rest", half(2), vmem(middle_b, wu0, wd0, gains), [], 0, 4_000_000_000)
    z_b, z_ra, wo1, wu1, wd1 = call(
        third_kernel, "shifted_attention", half(2) + FINISH,
        [(edge, pltpu.SMEM)] + vmem(normed_b, normed_ra, halo_b, halo_ra) + hbm(w_qkv, w_out, w_up, w_down),
        attention_scratch(1152) + QKV, 4, 4_000_000_000)
    att_a = ring(z_ra, "lon", 1)
    out_b, mg, wm = call(
        fourth_kernel, "block_two_rest", [jax.ShapeDtypeStruct((3, 9, LEV, 1024), BF16)] + MERGE,
        vmem(first_b, z_b, wo1, wu1, wd1, gains) + hbm(merge_gain.reshape(1, -1), w_merge), [], 2, 5_000_000_000)
    out, = call(
        fifth_kernel, "merge", [jax.ShapeDtypeStruct((6, 9, LEV, 1024), BF16)],
        vmem(first_a, att_a, out_b, wo1, wu1, wd1, gains, mg, wm), [], 0, 5_000_000_000)
    return out


def solution(mesh):
    return jax.shard_map(
        body,
        mesh=mesh,
        in_specs=(P("lon", "lat", None, None), P(), P(), P(), P(), P(), P(), P()),
        out_specs=P("lon", "lat", None, None),
        check_vma=False,
    )
```
